128 devices in a mesh: comp: 2 (over core), band: 32 (over z, x, y_hi), ch: 2 (over y_lo).
Axes of the slice: x: 4, y: 4 (y_hi: 2, y_lo: 2; y = y_hi * 2 + y_lo), z: 4, core: 2. Of those that a mesh axis runs over, the one named last changes fastest.
Arguments:
- air_initial: bfloat16 [128, 512, 768], P('band', 'comp', 'ch'), may hold values from -6 to 6
- sea_initial: bfloat16 [128, 512, 512], P('band', 'comp', 'ch'), may hold values from -6 to 6
- wet_dry_indicator: int32 [128, 512], P('band', 'comp'), may hold values 0 or 1
- regrid_source_boxes: int32 [4, 128, 512], P(None, 'band', 'comp'), may hold values from 0 to 65535, as said below
- air_layer_scales: float32 [2, 768], P(None, 'ch'), may hold values from 0.5 to 1.5
- air_layer_offsets: float32 [3, 768], P(None, 'ch'), may hold values from -4 to 4
- air_fourier_factors: float32 [4, 8, 96, 96], P(None, 'ch'), may hold values from -0.625 to 0.625
- air_fourier_offsets: float32 [4, 8, 96], P(None, 'ch'), may hold values from -4 to 4
- air_entry_matrix: bfloat16 [768, 3072], P(None, 'ch'), may hold values from -0.21875 to 0.21875
- air_inner_offset: bfloat16 [3072], P('ch'), may hold values from -4 to 4
- air_exit_matrix: bfloat16 [3072, 768], P('ch'), may hold values from -0.109375 to 0.109375
- sea_layer_scales: float32 [2, 512], P(None, 'ch'), may hold values from 0.5 to 1.5
- sea_layer_offsets: float32 [3, 512], P(None, 'ch'), may hold values from -4 to 4
- sea_fourier_factors: float32 [4, 8, 64, 64], P(None, 'ch'), may hold values from -0.75 to 0.75
- sea_fourier_offsets: float32 [4, 8, 64], P(None, 'ch'), may hold values from -4 to 4
- sea_entry_matrix: bfloat16 [512, 2048], P(None, 'ch'), may hold values from -0.25 to 0.25
- sea_inner_offset: bfloat16 [2048], P('ch'), may hold values from -4 to 4
- sea_exit_matrix: bfloat16 [2048, 512], P('ch'), may hold values from -0.125 to 0.125
- air_exchange_matrix: float32 [768, 4], P('ch'), may hold values from -0.21875 to 0.21875
- exchange_into_sea: float32 [4, 512], P(None, 'ch'), may hold values from -3 to 3
- skin_warmth_matrix: float32 [512], P('ch'), may hold values from -0.25 to 0.25
- warmth_into_air: float32 [768], P('ch'), may hold values from -6 to 6
Outputs:
- atmosphere_next: bfloat16 [128, 512, 768], P('band', 'comp', 'ch')
- ocean_next: bfloat16 [128, 512, 512], P('band', 'comp', 'ch')
The draws below stay inside these ranges and needn't reach their ends.
Inputs may be any that keep to these rules, and one draw needn't show every extreme that they name: `regrid_source_boxes`: each index names an atmosphere cell at most 2 rows away (rows clamped to the grid) and at most 2 columns away around the latitude circle; the first of the 4 indices of a cell is the cell itself.
All inputs are finite; a program needn't handle non-finite values. No bound on the sum of `wet_dry_indicator` on one device may be relied on, other than what follows from the above.
Results may differ from the reference program's by a relative error of at most 0.02.
Values may be sent and summed in bfloat16 or wider, within the bound.
No kernel may reach another device: no remote copies, remote signals or barrier semaphores. Data moves between devices by JAX's collectives and lax.ppermute only.
A program may use at most 128 MiB of HBM per device.

```python
import jax
import jax.numpy as jnp
from jax import lax

AIR_FEATURE_NUM = 768
SEA_FEATURE_NUM = 512
HID_A = 3072
HID_O = 2048
NB = 8
BSA = 96
BSO = 64
MERIDIAN_POINTS = 512
PARALLEL_LINES = 128
ATM_STEPS = 2
NF = 4
K = 4
RAD = 2


def draw_regrid_source_boxes(key, part):
    key = jax.random.fold_in(key, 7)
    key_rows, key_cols = jax.random.split(key)
    full_shape = (K, PARALLEL_LINES, MERIDIAN_POINTS)
    shift_rows = jax.random.randint(key_rows, full_shape, -RAD, RAD + 1)
    shift_cols = jax.random.randint(key_cols, full_shape, -RAD, RAD + 1)
    first_entry = (jnp.arange(K) == 0)[:, None, None]
    shift_rows = jnp.where(first_entry, 0, shift_rows)
    shift_cols = jnp.where(first_entry, 0, shift_cols)
    row_grid = jnp.arange(PARALLEL_LINES)[None, :, None]
    col_grid = jnp.arange(MERIDIAN_POINTS)[None, None, :]
    row_pick = jnp.clip(row_grid + shift_rows, 0, PARALLEL_LINES - 1)
    col_pick = (col_grid + shift_cols) % MERIDIAN_POINTS
    return (row_pick * MERIDIAN_POINTS + col_pick).astype(jnp.int32)


def with_ends(drawn, stream_key, least, largest):
    index_at = [jax.random.randint(jax.random.fold_in(stream_key, axis), (), 0, length) for axis, length in enumerate(drawn.shape)]
    widest = drawn.shape.index(max(drawn.shape))
    next_to = index_at[:widest] + [(index_at[widest] + 1) % drawn.shape[widest]] + index_at[widest + 1:]
    return drawn.at[tuple(index_at)].set(least).at[tuple(next_to)].set(largest)


def level_of(stream_key, shape, cuts, low, largest):
    level = 1.0
    for dim, blocks in cuts:
        steps = jax.random.uniform(jax.random.fold_in(jax.random.fold_in(stream_key, 6), dim), (blocks,), jnp.float32, low / len(cuts), largest / len(cuts))
        level = level * jnp.repeat(jnp.exp(steps), shape[dim] // blocks).reshape((-1,) + (1,) * (len(shape) - 1 - dim))
    return level


def scatter_about(stream_key, extent, spread, limit, shards=(), dtype=jnp.bfloat16):
    gain = level_of(stream_key, extent, shards, -0.22, 0.18) if shards else 1.0
    values = jax.random.normal(stream_key, extent, jnp.float32) * spread * gain
    return jnp.minimum(jnp.maximum(values, -limit), limit).astype(dtype)


def setup_inputs(seed: int = 0) -> dict:
    key_list = jax.random.split(jax.random.key(seed), 23)
    return {
        "air_initial": scatter_about(key_list[0], (PARALLEL_LINES, MERIDIAN_POINTS, AIR_FEATURE_NUM), 1.0, 6.0, ((0, 32), (1, 2), (2, 2))),
        "sea_initial": scatter_about(key_list[1], (PARALLEL_LINES, MERIDIAN_POINTS, SEA_FEATURE_NUM), 1.0, 6.0, ((0, 32), (1, 2), (2, 2))),
        "wet_dry_indicator": with_ends((jax.random.randint(key_list[2], (PARALLEL_LINES, MERIDIAN_POINTS), 0, 10) < 7).astype(jnp.int32), jax.random.fold_in(key_list[2], 1), 0, 1),
        "regrid_source_boxes": draw_regrid_source_boxes(jax.random.fold_in(key_list[22], 71), 0),
        "air_layer_scales": jnp.clip(1.0 + 0.1 * jax.random.normal(key_list[4], (2, AIR_FEATURE_NUM), jnp.float32), 0.5, 1.5),
        "air_layer_offsets": scatter_about(key_list[5], (3, AIR_FEATURE_NUM), 0.3, 4.0, ((1, 2),), jnp.float32),
        "air_fourier_factors": scatter_about(key_list[6], (4, NB, BSA, BSA), BSA ** -0.5, 0.625, ((1, 2),), jnp.float32),
        "air_fourier_offsets": scatter_about(key_list[7], (4, NB, BSA), 0.3, 4.0, ((1, 2),), jnp.float32),
        "air_entry_matrix": scatter_about(key_list[8], (AIR_FEATURE_NUM, HID_A), AIR_FEATURE_NUM ** -0.5, 0.21875, ((1, 2),)),
        "air_inner_offset": scatter_about(key_list[9], (HID_A,), 0.3, 4.0, ((0, 2),)),
        "air_exit_matrix": scatter_about(key_list[10], (HID_A, AIR_FEATURE_NUM), HID_A ** -0.5, 0.109375, ((0, 2),)),
        "sea_layer_scales": jnp.clip(1.0 + 0.1 * jax.random.normal(key_list[11], (2, SEA_FEATURE_NUM), jnp.float32), 0.5, 1.5),
        "sea_layer_offsets": scatter_about(key_list[12], (3, SEA_FEATURE_NUM), 0.3, 4.0, ((1, 2),), jnp.float32),
        "sea_fourier_factors": scatter_about(key_list[13], (4, NB, BSO, BSO), BSO ** -0.5, 0.75, ((1, 2),), jnp.float32),
        "sea_fourier_offsets": scatter_about(key_list[14], (4, NB, BSO), 0.3, 4.0, ((1, 2),), jnp.float32),
        "sea_entry_matrix": scatter_about(key_list[15], (SEA_FEATURE_NUM, HID_O), SEA_FEATURE_NUM ** -0.5, 0.25, ((1, 2),)),
        "sea_inner_offset": scatter_about(key_list[16], (HID_O,), 0.3, 4.0, ((0, 2),)),
        "sea_exit_matrix": scatter_about(key_list[17], (HID_O, SEA_FEATURE_NUM), HID_O ** -0.5, 0.125, ((0, 2),)),
        "air_exchange_matrix": scatter_about(key_list[18], (AIR_FEATURE_NUM, NF), AIR_FEATURE_NUM ** -0.5, 0.21875, ((0, 2),), jnp.float32),
        "exchange_into_sea": scatter_about(key_list[19], (NF, SEA_FEATURE_NUM), NF ** -0.5, 3.0, ((1, 2),), jnp.float32),
        "skin_warmth_matrix": scatter_about(key_list[20], (SEA_FEATURE_NUM,), SEA_FEATURE_NUM ** -0.5, 0.25, ((0, 2),), jnp.float32),
        "warmth_into_air": scatter_about(key_list[21], (AIR_FEATURE_NUM,), 1.0, 6.0, ((0, 2),), jnp.float32),
    }


epsilon = 1e-05
shrink_level = 0.01

def layer_norm(values, gain_row, shift_row):
    average = lax.optimization_barrier(jnp.mean(values, axis=-1, keepdims=True))
    square_mean = lax.optimization_barrier(jnp.mean(values * values, axis=-1, keepdims=True))
    return (values - average) * lax.rsqrt(square_mean - average * average + epsilon) * gain_row + shift_row

def soft_shrink(values):
    return values - jnp.clip(values, -shrink_level, shrink_level)

def block_mix(values, weight):
    return jnp.einsum('...nb,nbc->...nc', values, weight, precision=lax.Precision.HIGHEST)

def spectral_mix(real_part, imag_part, spec_weight, spec_bias):
    first_re = jax.nn.relu(block_mix(real_part, spec_weight[0]) - block_mix(imag_part, spec_weight[1]) + spec_bias[0])
    first_im = jax.nn.relu(block_mix(real_part, spec_weight[1]) + block_mix(imag_part, spec_weight[0]) + spec_bias[1])
    second_re = block_mix(first_re, spec_weight[2]) - block_mix(first_im, spec_weight[3]) + spec_bias[2]
    second_im = block_mix(first_re, spec_weight[3]) + block_mix(first_im, spec_weight[2]) + spec_bias[3]
    return (soft_shrink(second_re), soft_shrink(second_im))

def afno_block(present_variables, marine_box_share, gain_rows, shift_rows, spec_weight, spec_bias, w_in, b_in, w_out):
    rows_all, cols_all, width = present_variables.shape
    normed = layer_norm(present_variables, gain_rows[0], shift_rows[0])
    if marine_box_share is not None:
        normed = normed * marine_box_share[..., None]
    normed = normed.astype(jnp.bfloat16)
    lon_spec = jnp.fft.fft(normed.astype(jnp.float32), axis=1, norm='ortho')
    spec_re = lon_spec.real.astype(jnp.bfloat16).astype(jnp.float32)
    spec_im = lon_spec.imag.astype(jnp.bfloat16).astype(jnp.float32)
    modes = jnp.fft.fft(spec_re + 1j * spec_im, axis=0, norm='ortho')
    blocks = spec_weight.shape[1]
    mix_re, mix_im = spectral_mix(modes.real.reshape(rows_all, cols_all, blocks, -1), modes.imag.reshape(rows_all, cols_all, blocks, -1), spec_weight, spec_bias)
    mix_re = mix_re.reshape(rows_all, cols_all, width)
    mix_im = mix_im.reshape(rows_all, cols_all, width)
    lat_back = jnp.fft.ifft(mix_re + 1j * mix_im, axis=0, norm='ortho')
    back_re = lat_back.real.astype(jnp.bfloat16).astype(jnp.float32)
    back_im = lat_back.imag.astype(jnp.bfloat16).astype(jnp.float32)
    spatial = jnp.fft.ifft(back_re + 1j * back_im, axis=1, norm='ortho').real
    mixed_state = present_variables + spatial
    normed_two = layer_norm(mixed_state, gain_rows[1], shift_rows[1]).astype(jnp.bfloat16).reshape(-1, width)
    hidden = jax.nn.gelu(jnp.dot(normed_two, w_in, preferred_element_type=jnp.float32) + b_in.astype(jnp.float32))
    hidden = hidden.astype(jnp.bfloat16)
    result = jnp.dot(hidden, w_out, preferred_element_type=jnp.float32).reshape(rows_all, cols_all, width)
    return mixed_state + (result + shift_rows[2])

def reference(air_initial, sea_initial, wet_dry_indicator, regrid_source_boxes, air_layer_scales, air_layer_offsets, air_fourier_factors, air_fourier_offsets, air_entry_matrix, air_inner_offset, air_exit_matrix, sea_layer_scales, sea_layer_offsets, sea_fourier_factors, sea_fourier_offsets, sea_entry_matrix, sea_inner_offset, sea_exit_matrix, air_exchange_matrix, exchange_into_sea, skin_warmth_matrix, warmth_into_air):
    marine_box_share = wet_dry_indicator.astype(jnp.float32)
    marine_box_amounts = sea_initial.astype(jnp.float32)
    skin_warmth_grid = jnp.dot(marine_box_amounts.reshape(-1, SEA_FEATURE_NUM), skin_warmth_matrix, precision=lax.Precision.HIGHEST).reshape(PARALLEL_LINES, MERIDIAN_POINTS)
    present_variables = air_initial.astype(jnp.float32) + (marine_box_share * skin_warmth_grid)[..., None] * warmth_into_air
    flux_total = jnp.zeros((PARALLEL_LINES * MERIDIAN_POINTS, NF), jnp.float32)
    stored = air_initial
    for step_index in range(ATM_STEPS):
        stored = afno_block(present_variables, None, air_layer_scales, air_layer_offsets, air_fourier_factors, air_fourier_offsets, air_entry_matrix, air_inner_offset, air_exit_matrix).astype(jnp.bfloat16)
        flux_total = flux_total + jnp.dot(stored.astype(jnp.float32).reshape(-1, AIR_FEATURE_NUM), air_exchange_matrix, precision=lax.Precision.HIGHEST)
        present_variables = stored.astype(jnp.float32)
    average = flux_total / ATM_STEPS
    picked = jnp.take(average, regrid_source_boxes.reshape(-1).astype(jnp.int32), axis=0).reshape(K, PARALLEL_LINES, MERIDIAN_POINTS, NF)
    regridded = lax.optimization_barrier(jnp.mean(picked, axis=0))
    ocean_input = marine_box_amounts + jnp.dot(regridded.reshape(-1, NF), exchange_into_sea, precision=lax.Precision.HIGHEST).reshape(PARALLEL_LINES, MERIDIAN_POINTS, SEA_FEATURE_NUM)
    ocean_out = afno_block(ocean_input, marine_box_share, sea_layer_scales, sea_layer_offsets, sea_fourier_factors, sea_fourier_offsets, sea_entry_matrix, sea_inner_offset, sea_exit_matrix).astype(jnp.bfloat16)
    ocean_out = ocean_out * wet_dry_indicator.astype(jnp.bfloat16)[..., None]
    return (stored, ocean_out)
```

```python
import functools
import math

import jax
import jax.numpy as jnp
import ml_dtypes
import numpy as np
from jax import lax
from jax.experimental import pallas as pl
from jax.experimental.pallas import tpu as pltpu
from jax.sharding import Mesh, PartitionSpec as P


ROWS = 128
LONS = 512
EPS = 1e-05
SHRINK = 0.01
F32 = jnp.float32
BF16 = jnp.bfloat16
AXES = ("comp", "z", "x", "yh", "yl")
ROW_AXES = ("z", "x", "yh", "comp", "yl")
QUAD = ("comp", "yl")


def lon_table():
    slot = np.arange(LONS // 2)
    w = np.arange(LONS)
    phase = 2.0 * np.pi * ((slot[:, None] * w[None, :]) % LONS) / LONS
    f = np.stack([np.cos(phase), -np.sin(phase)], axis=1)
    f[0, 1] = np.where(w % 2 == 0, 1.0, -1.0)
    f = f.reshape(ROWS, 4, LONS) / math.sqrt(LONS)
    t = np.zeros((ROWS, 2, 4, 2, LONS))
    for q in range(2):
        t[:, q, :, q, :] = f
    return t.reshape(ROWS * 8, 2 * LONS)


def lat_tables():
    m = np.arange(ROWS)
    phase = 2.0 * np.pi * ((m[:, None] * m[None, :]) % ROWS) / ROWS
    c = np.cos(phase) / math.sqrt(ROWS)
    s = np.sin(phase) / math.sqrt(ROWS)
    t = np.zeros((2, 2, 6, ROWS, ROWS, 2, 2, 2))
    for kind in range(2):
        for q in range(2):
            if kind == 0:
                t[kind, q, 0, :, :, q, 0, 0] = c
                t[kind, q, 0, :, :, q, 0, 1] = s
                t[kind, q, 1, :, :, q, 0, 0] = -s
                t[kind, q, 1, :, :, q, 0, 1] = c
                t[kind, q, 2] = t[kind, q, 0]
                t[kind, q, 3] = -t[kind, q, 1]
            else:
                t[kind, q, 0, :, :, q, 0, 0] = c
                t[kind, q, 1, :, :, q, 0, 0] = -s
                t[kind, q, 2, :, :, q, 0, 1] = c
                t[kind, q, 3, :, :, q, 0, 1] = -s
            t[kind, q, 4, :, :, q, 1, 0] = c
            t[kind, q, 4, :, :, q, 1, 1] = s
            t[kind, q, 5, :, :, q, 1, 0] = -s
            t[kind, q, 5, :, :, q, 1, 1] = c
    t = t.reshape(2, 2, 6 * ROWS, ROWS * 8)
    return t, np.swapaxes(t, 2, 3)


def as_bf16(table):
    return jnp.asarray(np.ascontiguousarray(table).astype(ml_dtypes.bfloat16))


def mm(a, b):
    return jnp.dot(a, b, preferred_element_type=F32)


def norm(v, g, b):
    n = v.shape[1]
    m = jnp.sum(v, axis=1, keepdims=True) / n
    q = jnp.sum(v * v, axis=1, keepdims=True) / n
    return (v - m) * lax.rsqrt(q - m * m + EPS) * g + b


def stack_halves(x):
    half = x.shape[1] // 2
    return jnp.concatenate([x[:, :half], x[:, half:]], axis=0)


def from_quad(ref):
    return jnp.concatenate(
        [jnp.concatenate([ref[2 * c], ref[2 * c + 1]], axis=1) for c in range(2)], axis=0
    )


def to_quad(ref, x):
    w, half = x.shape[0] // 2, x.shape[1] // 2
    for c in range(2):
        for h in range(2):
            ref[2 * c + h] = x[c * w:(c + 1) * w, h * half:(h + 1) * half]


def aux_row(aux_ref, i):
    return jnp.concatenate([aux_ref[0, i:i + 1], aux_ref[2, i:i + 1]], axis=1)


def column(row):
    return jnp.transpose(jnp.broadcast_to(row, (8, row.shape[1])))[:, 0:1]


def start_kernel(air_ref, aux_ref, warm_ref, g_ref, b_ref, tf_ref, x_ref, v_ref):
    sst = aux_row(aux_ref, 0) + jnp.concatenate([aux_ref[1, 0:1], aux_ref[3, 0:1]], axis=1)
    v = from_quad(air_ref).astype(F32) + column(sst * aux_row(aux_ref, 1)) * warm_ref[...]
    v_ref[...] = v
    n = norm(v, g_ref[...], b_ref[...]).astype(BF16)
    x_ref[...] = mm(tf_ref[...], stack_halves(n)).astype(BF16)


def modes_kernel(dev_ref, x_ref, tl_ref, ti_ref, w1_ref, w2_ref, c1_ref, c2_ref, o_ref, acc_ref):
    q = pl.program_id(0)
    half = x_ref.shape[1]
    y = mm(tl_ref[...], x_ref[...]).astype(BF16)
    part = lambda i: y[i * ROWS:(i + 1) * ROWS]
    z = jnp.concatenate(
        [
            jnp.concatenate([part(0), part(1)], axis=1),
            jnp.concatenate([part(2), part(3)], axis=1),
            jnp.concatenate([part(4), part(5)], axis=1),
            jnp.concatenate([part(4), -part(5)], axis=1),
        ],
        axis=0,
    )
    o1 = jax.nn.relu(mm(z, w1_ref[...]) + c1_ref[...]).astype(BF16)
    o2 = mm(o1, w2_ref[...]) + c2_ref[...]
    f = o2 - jnp.clip(o2, -SHRINK, SHRINK)
    fr, fi = f[:, :half], f[:, half:]
    block = lambda a, i: a[i * ROWS:(i + 1) * ROWS]
    h = jnp.concatenate(
        [
            block(fr, 0),
            block(fi, 0),
            block(fr, 1),
            block(fi, 1),
            block(fr, 2) + block(fr, 3),
            block(fi, 2) - block(fi, 3),
        ],
        axis=0,
    ).astype(BF16)
    back = mm(ti_ref[...], h)

    @pl.when(q == 0)
    def _():
        acc_ref[...] = back

    @pl.when(q == 1)
    def _():
        o_ref[...] = (acc_ref[...] + back).astype(BF16)


def grid_kernel(kind, *refs):
    refs = list(refs)
    x_ref, v_ref, ti_ref, g_ref, b_ref, win_ref, bin_ref, wout_ref = refs[:8]
    refs = refs[8:]
    if kind == "sea":
        aux_ref = refs.pop(0)
    else:
        e_ref = refs.pop(0)
        if kind == "first":
            tf_ref = refs.pop(0)
    s_ref = refs.pop(0)
    if kind != "sea":
        flux_ref = refs.pop(0)
    if kind == "first":
        xo_ref = refs.pop(0)
    mixed_ref, n2_ref, acc_ref = refs
    step = pl.program_id(0)

    @pl.when(step == 0)
    def _():
        both = mm(ti_ref[...], x_ref[...])
        spatial = jnp.concatenate([both[:LONS], both[LONS:]], axis=1)
        v = from_quad(v_ref).astype(F32) if kind == "second" else v_ref[...]
        mixed = v + spatial
        mixed_ref[...] = mixed
        n2_ref[...] = norm(mixed, g_ref[1:2], b_ref[1:2]).astype(BF16)
        acc_ref[...] = jnp.zeros_like(acc_ref)

    width = win_ref.shape[0] * win_ref.shape[1]
    w_in = win_ref[...].reshape(width, -1)
    hid = w_in.shape[1]
    w_out = wout_ref[...].reshape(hid, width)
    piece = 512
    for i in range(hid // piece):
        cols = slice(i * piece, (i + 1) * piece)
        pre = mm(n2_ref[...], w_in[:, cols]) + bin_ref[:, cols]
        acc_ref[...] += mm(jax.nn.gelu(pre).astype(BF16), w_out[cols])

    @pl.when(step == pl.num_programs(0) - 1)
    def _():
        s = (mixed_ref[...] + (acc_ref[...] + b_ref[2:3])).astype(BF16)
        if kind == "sea":
            to_quad(s_ref, (s.astype(F32) * column(aux_row(aux_ref, 1))).astype(BF16))
            return
        to_quad(s_ref, s)
        e = e_ref[...]
        e0 = e.astype(BF16)
        r = e - e0.astype(F32)
        e1 = r.astype(BF16)
        e2 = (r - e1.astype(F32)).astype(BF16)
        fl = lax.dot_general(
            jnp.concatenate([e0, e1, e2], axis=0), s, (((1,), (1,)), ((), ())),
            preferred_element_type=F32,
        )
        flux_ref[...] = (fl[0:16] + fl[16:32] + fl[32:48])[0:8]
        if kind == "first":
            n = norm(s.astype(F32), g_ref[0:1], b_ref[0:1]).astype(BF16)
            xo_ref[...] = mm(tf_ref[...], stack_halves(n)).astype(BF16)


def sea_kernel(dev_ref, flux_ref, aux_ref, sea_ref, ex_ref, g_ref, b_ref, tf_ref, x_ref, v_ref):
    r = dev_ref[0]
    boxes = jnp.concatenate([aux_ref[0, 2:6], aux_ref[2, 2:6]], axis=1).astype(jnp.int32)
    dr = (boxes >> 9) - r + 2
    here = lax.broadcasted_iota(jnp.int32, boxes.shape, 1)
    dc = ((boxes & (LONS - 1)) - here + (2 + LONS)) & (LONS - 1)
    where = dr * 8 + dc
    total = jnp.zeros((8, LONS), F32)
    for i in range(5):
        for j in range(5):
            hits = jnp.sum(jnp.where(where == i * 8 + j, 1.0, 0.0), axis=0, keepdims=True)
            total = total + hits * pltpu.roll(flux_ref[i], (2 - j) % LONS, 1)
    cols = jnp.transpose(total * 0.25)
    v = from_quad(sea_ref).astype(F32)
    for f in range(4):
        v = v + cols[:, f:f + 1] * ex_ref[f:f + 1]
    v_ref[...] = v
    wet = column(aux_row(aux_ref, 1))
    n = (norm(v, g_ref[0:1], b_ref[0:1]) * wet).astype(BF16)
    x_ref[...] = mm(tf_ref[...], stack_halves(n)).astype(BF16)


PARAMS = dict(vmem_limit_bytes=50 * 1024 * 1024)
VM = pl.BlockSpec(memory_space=pltpu.VMEM)
SM = pl.BlockSpec(memory_space=pltpu.SMEM)


def shape(dims, dtype):
    return jax.ShapeDtypeStruct(dims, dtype)


def cost(flops, bytes_accessed, tr=0):
    return pl.CostEstimate(flops=flops, bytes_accessed=bytes_accessed, transcendentals=tr)


def run_modes(dev, x, tl, ti, w1, w2, c1, c2):
    half = x.shape[1]
    two = 2 * half
    k = 6 * ROWS
    kind = lambda q, d: (jnp.where(d[0] == 0, 1, 0), q, 0, 0)
    part = lambda q, d: (q, 0, 0)
    whole = lambda q, d: (0, 0)
    sq = pl.Squeezed()
    return pl.pallas_call(
        modes_kernel,
        out_shape=shape((8 * ROWS, half), BF16),
        grid_spec=pltpu.PrefetchScalarGridSpec(
            num_scalar_prefetch=1,
            grid=(2,),
            in_specs=[
                pl.BlockSpec((8 * ROWS, half), whole),
                pl.BlockSpec((sq, sq, k, 8 * ROWS), kind),
                pl.BlockSpec((sq, sq, 8 * ROWS, k), kind),
                pl.BlockSpec((sq, two, two), part),
                pl.BlockSpec((sq, two, two), part),
                pl.BlockSpec((sq, 1, two), part),
                pl.BlockSpec((sq, 1, two), part),
            ],
            out_specs=pl.BlockSpec((8 * ROWS, half), whole),
            scratch_shapes=[pltpu.VMEM((8 * ROWS, half), F32)],
        ),
        compiler_params=pltpu.CompilerParams(**PARAMS),
        cost_estimate=cost(4 * 8 * ROWS * k * half * 2 // 2 + 8 * 512 * two * two, 12_000_000),
        name="modes",
    )(dev, x, tl, ti, w1, w2, c1, c2)


def run_grid(kind, x, v, ti, g, b, w_in, b_in, w_out, *rest):
    half = x.shape[1]
    width = 2 * half
    hid = b_in.shape[2]
    full = lambda a: pl.BlockSpec(a.shape, lambda i, n=a.ndim: (0,) * n)
    sq = pl.Squeezed()
    outs = [shape((4, LONS // 2, half), BF16)]
    if kind != "sea":
        outs.append(shape((8, LONS), F32))
    if kind == "first":
        outs.append(shape((8 * ROWS, half), BF16))
    return pl.pallas_call(
        functools.partial(grid_kernel, kind),
        out_shape=tuple(outs),
        grid=(2,),
        in_specs=[
            full(x), full(v), full(ti), full(g), full(b),
            pl.BlockSpec((4, sq, width // 4, hid), lambda i: (0, i, 0, 0)),
            pl.BlockSpec((sq, 1, hid), lambda i: (i, 0, 0)),
            pl.BlockSpec((4, sq, hid // 4, width), lambda i: (0, i, 0, 0)),
            *[full(a) for a in rest],
        ],
        out_specs=tuple(full(o) for o in outs),
        scratch_shapes=[
            pltpu.VMEM((LONS, width), F32),
            pltpu.VMEM((LONS, width), BF16),
            pltpu.VMEM((LONS, width), F32),
        ],
        compiler_params=pltpu.CompilerParams(**PARAMS),
        cost_estimate=cost(8 * LONS * width * hid, 16_000_000, LONS * 2 * hid),
        name="grid_" + kind,
    )(x, v, ti, g, b, w_in, b_in, w_out, *rest)


def block_diag(w):
    n, k, _ = w.shape
    spread = jnp.where(jnp.eye(n, dtype=bool)[:, None, :, None], w[:, :, None, :], 0)
    return spread.reshape(n * k, n * k)


def mode_weights(spec):
    def pair(re, im):
        return jnp.concatenate(
            [jnp.concatenate([re, im], axis=1), jnp.concatenate([-im, re], axis=1)], axis=0
        )

    every = lax.all_gather(spec.astype(BF16), "yl", axis=0)
    parts = [[block_diag(every[q, i]) for i in range(4)] for q in range(2)]
    return (
        jnp.stack([pair(p[0], p[1]) for p in parts]),
        jnp.stack([pair(p[2], p[3]) for p in parts]),
    )


def gather_weights(w_in, w_out):
    place = lax.axis_index("comp") * 2 + lax.axis_index("yh")
    axes = ("comp", "yh", "yl")
    rows = w_in.shape[0] // 4
    one = lax.dynamic_slice_in_dim(w_in, place * rows, rows, axis=0)
    one = lax.all_gather(one, axes, axis=0).reshape(4, 2, rows, w_in.shape[1])
    rows = w_out.shape[0] // 4
    two = lax.dynamic_slice_in_dim(w_out, place * rows, rows, axis=0)
    two = lax.all_gather(two, axes, axis=0).reshape(4, 2, rows, w_out.shape[1])
    return one, two


def spread(x):
    half = x.shape[1]
    y = lax.all_to_all(x.reshape(ROWS, 8, half), ROW_AXES, 0, 0, tiled=True)
    return y.reshape(8 * ROWS, half)


def row_shift(x, by):
    def place(r):
        return (r // 2 % 2) * (ROWS // 2) + (r // 4) * 2 + r % 2

    return lax.ppermute(x, AXES, [(place(r), place((r + by) % ROWS)) for r in range(ROWS)])


def per_device(
    air, sea, wet, boxes,
    a_gain, a_shift, a_spec, a_sbias, a_win, a_bin, a_wout,
    s_gain, s_shift, s_spec, s_sbias, s_win, s_bin, s_wout,
    air_ex, sea_ex, skin, warm,
):
    tl, ti = (as_bf16(t) for t in lat_tables())
    table = lon_table()
    tf, tfi = as_bf16(table), as_bf16(table.T)
    row = lax.axis_index(ROW_AXES).astype(jnp.int32).reshape(1)

    sst = jnp.einsum("jgo,o->jg", sea.astype(F32), skin, precision=lax.Precision.HIGHEST)
    aux = jnp.concatenate(
        [
            sst[:, None],
            wet.astype(F32)[:, None],
            jnp.transpose(boxes, (1, 0, 2)).astype(F32),
            jnp.zeros((4, 2, LONS // 2), F32),
        ],
        axis=1,
    )
    aux = lax.all_to_all(aux, QUAD, 0, 0, tiled=True)
    air_rows = lax.all_to_all(air, QUAD, 0, 0, tiled=True)

    small = [
        a_gain, a_shift, a_sbias.reshape(4, -1), a_bin.astype(F32).reshape(1, -1),
        jnp.transpose(air_ex), warm[None],
        s_gain, s_shift, s_sbias.reshape(4, -1), s_bin.astype(F32).reshape(1, -1), sea_ex,
    ]
    flat = jnp.concatenate([p.reshape(-1) for p in small])
    flat = lax.all_gather(flat, "yl", axis=0)
    full, at = [], 0
    for p in small:
        piece = flat[:, at:at + p.size].reshape(2, p.shape[0], p.shape[1])
        full.append(piece)
        at += p.size
    wide = lambda p: jnp.transpose(p, (1, 0, 2)).reshape(p.shape[1], -1)
    ag, ash, asb, ab, ae, aw, sg, ssh, ssb, sb, se = full
    ag, ash, ae, aw, sg, ssh, se = (wide(p) for p in (ag, ash, ae, aw, sg, ssh, se))
    ae = jnp.concatenate([ae, jnp.zeros((12, ae.shape[1]), F32)], axis=0)
    biases = lambda p: (p[:, 0:2].reshape(2, 1, -1), p[:, 2:4].reshape(2, 1, -1))
    ac1, ac2 = biases(asb)
    sc1, sc2 = biases(ssb)

    aw1, aw2 = mode_weights(a_spec)
    awin, awout = gather_weights(a_win, a_wout)
    sea_rows = lax.all_to_all(sea, QUAD, 0, 0, tiled=True)
    sw1, sw2 = mode_weights(s_spec)
    swin, swout = gather_weights(s_win, s_wout)

    half = air.shape[2]
    x, v = pl.pallas_call(
        start_kernel,
        out_shape=(shape((8 * ROWS, half), BF16), shape((LONS, 2 * half), F32)),
        in_specs=[VM] * 6,
        out_specs=(VM, VM),
        compiler_params=pltpu.CompilerParams(**PARAMS),
        cost_estimate=cost(2 * 1024 * 1024 * half, 6_000_000),
        name="start",
    )(air_rows, aux, aw, ag[0:1], ash[0:1], tf)

    x = spread(x)
    x = run_modes(row, x, tl, ti, aw1, aw2, ac1, ac2)
    x = spread(x)
    s, flux_one, x = run_grid("first", x, v, tfi, ag, ash, awin, ab, awout, ae, tf)
    x = spread(x)
    x = run_modes(row, x, tl, ti, aw1, aw2, ac1, ac2)
    x = spread(x)
    s, flux_two = run_grid("second", x, s, tfi, ag, ash, awin, ab, awout, ae)
    air_out = lax.all_to_all(s, QUAD, 0, 0, tiled=True)

    flux = (flux_one + flux_two) / 2
    fluxes = jnp.stack(
        [row_shift(flux, 2), row_shift(flux, 1), flux, row_shift(flux, -1), row_shift(flux, -2)]
    )
    half = sea.shape[2]
    x, v = pl.pallas_call(
        sea_kernel,
        out_shape=(shape((8 * ROWS, half), BF16), shape((LONS, 2 * half), F32)),
        in_specs=[SM] + [VM] * 7,
        out_specs=(VM, VM),
        compiler_params=pltpu.CompilerParams(**PARAMS),
        cost_estimate=cost(2 * 1024 * 1024 * half, 5_000_000),
        name="sea_start",
    )(row, fluxes, aux, sea_rows, se, sg, ssh, tf)
    x = spread(x)
    x = run_modes(row, x, tl, ti, sw1, sw2, sc1, sc2)
    x = spread(x)
    (s,) = run_grid("sea", x, v, tfi, sg, ssh, swin, sb, swout, aux)
    sea_out = lax.all_to_all(s, QUAD, 0, 0, tiled=True)
    return air_out, sea_out


def solution(mesh):
    fine = Mesh(mesh.devices.reshape(2, 4, 4, 2, 2), AXES)
    band = ("z", "x", "yh")
    placed = (
        P(band, "comp", "yl"),
        P(band, "comp", "yl"),
        P(band, "comp"),
        P(None, band, "comp"),
        P(None, "yl"),
        P(None, "yl"),
        P(None, "yl", None, None),
        P(None, "yl", None),
        P(None, "yl"),
        P("yl"),
        P("yl", None),
        P(None, "yl"),
        P(None, "yl"),
        P(None, "yl", None, None),
        P(None, "yl", None),
        P(None, "yl"),
        P("yl"),
        P("yl", None),
        P("yl", None),
        P(None, "yl"),
        P("yl"),
        P("yl"),
    )
    return jax.shard_map(
        per_device,
        mesh=fine,
        in_specs=placed,
        out_specs=(P(band, "comp", "yl"), P(band, "comp", "yl")),
        check_vma=False,
    )
```

```python
import functools
import math

import jax
import jax.numpy as jnp
import ml_dtypes
import numpy as np
from jax import lax
from jax.experimental import pallas as pl
from jax.experimental.pallas import tpu as pltpu
from jax.sharding import Mesh, PartitionSpec as P


ROWS = 128
LONS = 512
EPS = 1e-05
SHRINK = 0.01
F32 = jnp.float32
BF16 = jnp.bfloat16
AXES = ("comp", "z", "x", "yh", "yl")
ROW_AXES = ("z", "x", "yh", "comp", "yl")
QUAD = ("comp", "yl")

AIR_G, AIR_S, AIR_C, AIR_E, AIR_W, AIR_B = 0, 2, 5, 9, 13, 14
SEA_G, SEA_S, SEA_C, SEA_E, SEA_B = 18, 20, 23, 27, 31
WET, BOX, PACKED = 35, 36, 40
PLUS = 16


def lon_table():
    slot = np.arange(LONS // 2)
    w = np.arange(LONS)
    phase = 2.0 * np.pi * ((slot[:, None] * w[None, :]) % LONS) / LONS
    f = np.stack([np.cos(phase), -np.sin(phase)], axis=1)
    f[0, 1] = np.where(w % 2 == 0, 1.0, -1.0)
    f = f.reshape(ROWS, 4, LONS) / math.sqrt(LONS)
    return np.swapaxes(f, 0, 1).reshape(4 * ROWS, LONS)


def lat_tables():
    m = np.arange(ROWS)
    phase = 2.0 * np.pi * ((m[:, None] * m[None, :]) % ROWS) / ROWS
    c = np.cos(phase) / math.sqrt(ROWS)
    s = np.sin(phase) / math.sqrt(ROWS)
    o = np.zeros_like(c)
    usual = np.block([[c, s], [-s, c]])
    conj = np.block([[c, s], [s, -c]])
    first = np.stack(
        [np.concatenate([usual, conj]), np.block([[c, o], [-s, o], [o, c], [o, -s]])]
    )
    back = np.swapaxes(first, 1, 2)
    halves = np.stack([back[:, :, :256], back[:, :, 256:]], axis=1)
    return np.concatenate([first.reshape(-1, 256), halves.reshape(-1, 256), usual, usual.T])


def as_bf16(table):
    return jnp.asarray(np.ascontiguousarray(table).astype(ml_dtypes.bfloat16))


def mm(a, b):
    return jnp.dot(a, b, preferred_element_type=F32)


def norm(v, g, b):
    n = v.shape[1]
    m = jnp.sum(v, axis=1, keepdims=True) / n
    q = jnp.sum(v * v, axis=1, keepdims=True) / n
    return (v - m) * lax.rsqrt(q - m * m + EPS) * g + b


def from_quad(ref):
    return jnp.concatenate(
        [jnp.concatenate([ref[2 * c], ref[2 * c + 1]], axis=1) for c in range(2)], axis=0
    )


def to_quad(ref, x):
    w, half = x.shape[0] // 2, x.shape[1] // 2
    for c in range(2):
        for h in range(2):
            ref[2 * c + h] = x[c * w:(c + 1) * w, h * half:(h + 1) * half]


def wide(p_ref, i, half):
    return jnp.concatenate([p_ref[0, i:i + 1, :half], p_ref[1, i:i + 1, :half]], axis=1)


def along(p_ref, i, n=1):
    return jnp.concatenate([p_ref[0, i:i + n, :LONS // 2], p_ref[1, i:i + n, :LONS // 2]], axis=1)


def column(row):
    return jnp.transpose(jnp.broadcast_to(row, (8, row.shape[1])))[:, 0:1]


def to_chunks(tf_ref, n, scratch, put, i):
    half = n.shape[1] // 2
    for q in range(2):
        out = mm(tf_ref[:LONS], n[:, q * half:(q + 1) * half])
        for j in range(4):
            put_rows(scratch, 4 * q + j, out[j * ROWS:(j + 1) * ROWS])
    pour(put, i, scratch)


def put_rows(scratch, j, value):
    for t in range(scratch.shape[0]):
        scratch[t, pl.ds(j, ROWS, stride=8), :] = value[:, t * 128:(t + 1) * 128]


def pour(put, i, scratch):
    buf = put(i)
    moves = []
    for t in range(scratch.shape[0]):
        cols = slice(t * 128, (t + 1) * 128)
        buf[:, cols] = scratch[t].astype(BF16)
        moves.append(pltpu.make_async_copy(
            buf.at[:, pl.ds(t * 128, 128)], put.raw(i).at[:, pl.ds(t * 128, 128)], put.sem(8 + t)
        ))
        moves[-1].start()
    for m in moves:
        m.wait()


def fill(scratch, x_ref):
    for t in range(scratch.shape[0]):
        scratch[t] = x_ref[:, t * 128:(t + 1) * 128].astype(F32)


def rows_of(scratch, q, js):
    def one(j):
        return jnp.concatenate(
            [scratch[t, pl.ds(4 * q + j, ROWS, stride=8), :] for t in range(scratch.shape[0])], axis=1
        )

    return jnp.concatenate([one(j) for j in js], axis=0).astype(BF16)


def thirds(x):
    a = x.astype(BF16)
    r = x - a.astype(F32)
    b = r.astype(BF16)
    return a, b, (r - b.astype(F32)).astype(BF16)


def pack_kernel(get, put, scratch):
    out_hbm, (plus, sems) = put.raw(0), scratch
    air = get(0)
    n = air.shape[1]
    first = pltpu.make_async_copy(air, out_hbm.at[:, pl.ds(0, n)], sems.at[0])
    first.start()
    comp = lax.axis_index("comp")
    spec, part = put(1), put(2)
    spec[...] = jnp.zeros_like(spec)
    for src, top, k in ((5, 0, 96), (6, 384, 64)):
        for i in range(4):
            for j in range(4):
                spec[i, top + k * j:top + k * (j + 1), :k] = get(src)[i, j].astype(BF16)
    part[...] = spec[pl.ds(2 * comp, 2)]
    put.send(1, wait=False)
    put.send(2, wait=False)
    skin = jnp.concatenate([*thirds(get(2)[...]), jnp.zeros((13, get(2).shape[1]), BF16)], axis=0)
    rest = jnp.concatenate([get.raw(3)[0:1], get.raw(7)[0:1], get.raw(8)[...]], axis=0)
    wet = get(4)[...].astype(F32)
    sea = get(1)
    half = rest.shape[1]
    pad = jnp.zeros((1, half - LONS // 2), F32)
    for r in range(4):
        t = lax.dot_general(skin, sea[r], (((1,), (1,)), ((), ())), preferred_element_type=F32)
        sst = jnp.concatenate([t[0:1] + t[1:2] + t[2:3], pad], axis=1)
        rows = jnp.concatenate([sst, jnp.concatenate([wet[r:r + 1], pad], axis=1), rest], axis=0)
        plus[r] = jnp.concatenate([*thirds(rows), jnp.zeros((1, half), BF16)], axis=0)
    last = pltpu.make_async_copy(plus, out_hbm.at[:, pl.ds(n, PLUS)], sems.at[1])
    last.start()
    last.wait()
    put.done(1)
    put.done(2)
    first.wait()


def plus_rows(air_ref, source):
    n = LONS // 2
    t = air_ref[source, n:n + PLUS].astype(F32)
    return t[0:5] + t[5:10] + t[10:15]


def air_state(air_ref):
    n = LONS // 2
    first = plus_rows(air_ref, 0)
    other = plus_rows(air_ref, 1)
    far = plus_rows(air_ref, 2)
    last = plus_rows(air_ref, 3)
    near_sst = (first[0:1, :n] + other[0:1, :n]) * first[1:2, :n]
    far_sst = (far[0:1, :n] + last[0:1, :n]) * far[1:2, :n]
    both = jnp.concatenate([first[2:5], other[2:5]], axis=1)
    air = jnp.concatenate(
        [jnp.concatenate([air_ref[2 * c, :n], air_ref[2 * c + 1, :n]], axis=1) for c in range(2)], axis=0
    )
    v = air.astype(F32) + column(jnp.concatenate([near_sst, far_sst], axis=1)) * both[2:3]
    return v, both


def start_kernel(get, put, scratch):
    v, both = air_state(get(0))
    n = norm(v, both[0:1], both[1:2]).astype(BF16)
    to_chunks(get(1), n, scratch[0], put, 0)


def weights_kernel(get, put, scratch):
    g_ref, near_ref, far_ref, aw_ref, sw_ref = get(1), get(2), get(3), put(0), put(1)
    comp, flip = get.raw(0)[0], get.raw(0)[1]
    for w_ref, top, k in ((aw_ref, 0, 96), (sw_ref, 384, 64)):
        half = 4 * k
        lane = lax.broadcasted_iota(jnp.int32, (128, half), 1)
        sub = lax.broadcasted_iota(jnp.int32, (128, half), 0)
        place = [jnp.where((lane == sub + k * n) & (sub < k), 1.0, 0.0).astype(BF16) for n in range(4)]
        for q in range(2):
            for layer in range(2):
                for part in range(2):
                    src = 2 * layer + part
                    own = g_ref[src, top:top + half]
                    far = jnp.where(
                        comp == layer, near_ref[part, top:top + half], far_ref[part, top:top + half]
                    )
                    here = jnp.where(flip == q, own, far)
                    block = jnp.concatenate(
                        [mm(here[k * n:k * (n + 1)], place[n]) for n in range(4)], axis=0
                    )
                    here = block.astype(BF16)
                    if part == 0:
                        w_ref[layer, q, :half, :half] = here
                        w_ref[layer, q, half:, half:] = here
                    else:
                        w_ref[layer, q, :half, half:] = here
                        w_ref[layer, q, half:, :half] = (-block).astype(BF16)
    put.send(0, wait=False)
    put.send(1)
    put.done(0)


def modes_kernel(first, get, put, scratch):
    dev_ref, x_ref = get.raw(0), get.raw(1)
    xs, os = scratch[:2]
    half = x_ref.shape[1]
    kind = jnp.where(dev_ref[0] == 0, 1, 0)
    t_buf, w_buf, t_sems, w_sems = scratch[2:]
    t_loads = []
    for i, (at, n) in enumerate(((512 * kind, 512), (2048, 256), (1024 + 512 * kind, 512), (2304, 256))):
        t_loads.append(pltpu.make_async_copy(
            get.raw(3).at[pl.ds(pl.multiple_of(at, 256), n)], t_buf.at[pl.ds((0, 512, 768, 1280)[i], n)],
            t_sems.at[i],
        ))
    loads = [
        [pltpu.make_async_copy(get.raw(4).at[i, q], w_buf.at[i, q], w_sems.at[2 * q + i]) for i in range(2)]
        for q in range(2)
    ]
    t_loads[0].start()
    t_loads[1].start()
    loads[0][0].start()
    fill(xs, get(1))
    t_loads[0].wait()
    t_loads[1].wait()
    t_loads[2].start()
    t_loads[3].start()
    loads[0][1].start()
    p_ref = get(2)
    for q in range(2):
        y0 = mm(t_buf[0:512], rows_of(xs, q, (0, 1))).astype(BF16)
        y1 = mm(t_buf[512:768], rows_of(xs, q, (2, 3))).astype(BF16)
        part = lambda y, i: y[i * ROWS:(i + 1) * ROWS]
        z = jnp.concatenate(
            [
                jnp.concatenate([part(y0, 0), part(y0, 1)], axis=1),
                jnp.concatenate([part(y0, 2), part(y0, 3)], axis=1),
                jnp.concatenate([part(y1, 0), part(y1, 1)], axis=1),
                jnp.concatenate([part(y1, 0), -part(y1, 1)], axis=1),
            ],
            axis=0,
        )
        bias = lambda i: jnp.concatenate(
            [p_ref[q, i:i + 1, :half], p_ref[q, i + 1:i + 2, :half]], axis=1
        )
        loads[q][0].wait()
        if q == 0:
            loads[1][0].start()
        o1 = jax.nn.relu(mm(z, w_buf[0, q]) + bias(first)).astype(BF16)
        loads[q][1].wait()
        if q == 0:
            loads[1][1].start()
            t_loads[2].wait()
            t_loads[3].wait()
        o2 = mm(o1, w_buf[1, q]) + bias(first + 2)
        f = o2 - jnp.clip(o2, -SHRINK, SHRINK)
        fr, fi = f[:, :half], f[:, half:]
        h0 = jnp.concatenate([part(fr, 0), part(fi, 0)], axis=0).astype(BF16)
        h2 = jnp.concatenate([part(fr, 1), part(fi, 1)], axis=0).astype(BF16)
        h1 = jnp.concatenate([part(fr, 2) + part(fr, 3), part(fi, 2) - part(fi, 3)], axis=0)
        b0 = mm(t_buf[768:1024], h0) + mm(t_buf[1024:1280], h2)
        b1 = mm(t_buf[1280:1536], h1.astype(BF16))
        for j, b in enumerate((part(b0, 0), part(b0, 1), part(b1, 0), part(b1, 1))):
            put_rows(os, 4 * q + j, b)
    pour(put, 0, os)


def grid_kernel(kind, get, put, scratch):
    place_ref, x_ref = get.raw(0), get.raw(1)
    xs, n2_ref, acc_ref, win_ref, wout_ref, sems = scratch
    half = x_ref.shape[1]
    width = 2 * half
    gains, shifts, bias = (SEA_G, SEA_S, SEA_B) if kind == "sea" else (AIR_G, AIR_S, AIR_B)
    comp, yl = place_ref[0], place_ref[1]
    piece = 512
    hid = win_ref.shape[2]
    pieces = hid // piece

    own, far = [], []
    for i, (buf, at) in enumerate(((win_ref, 5), (wout_ref, 8))):
        n = buf.shape[1] // 2
        part = lambda c: pl.ds(pl.multiple_of(c * n, n), n)
        own.append(pltpu.make_async_copy(get.raw(at), buf.at[0], sems.at[3 * i]))
        far.append([
            pltpu.make_async_copy(get.raw(at + 1), buf.at[1, part(comp)], sems.at[3 * i + 1]),
            pltpu.make_async_copy(get.raw(at + 2), buf.at[1, part(1 - comp)], sems.at[3 * i + 2]),
        ])

    get.start(2, 3)
    if kind == "sea":
        get.start(11)
    own[0].start()
    fill(xs, get(1))
    v_ref, p_ref, ti_ref = get(2), get(3), get(4)
    own[1].start()
    if kind == "first":
        v, _ = air_state(v_ref)
    elif kind == "second":
        v = from_quad(v_ref).astype(F32)
    else:
        v = sea_state(v_ref, get(11), p_ref)
    spatial = jnp.concatenate(
        [mm(ti_ref[LONS:], rows_of(xs, q, range(4))) for q in range(2)], axis=1
    )
    mixed = v + spatial
    n2_ref[...] = norm(mixed, wide(p_ref, gains + 1, half), wide(p_ref, shifts + 1, half)).astype(BF16)
    acc_ref[...] = mixed + wide(p_ref, shifts + 2, half)

    for h in range(2):
        if kind == "sea" and h == 1:
            through = pltpu.make_async_copy(get(12), put.raw(1), put.sem(1))
            through.start()
        source = yl if h == 0 else 1 - yl
        b_in = jnp.concatenate(
            [p_ref[source, bias + i:bias + i + 1, :hid // 4] for i in range(4)], axis=1
        )
        for i in range(pieces):
            cols = slice(i * piece, (i + 1) * piece)
            if i == 0:
                for m in far[0] if h else [own[0]]:
                    m.wait()
            pre = mm(n2_ref[...], win_ref[h, :, cols]) + b_in[:, cols]
            if i == 0:
                for m in far[1] if h else [own[1]]:
                    m.wait()
                if h == 0:
                    for m in [*far[0], *far[1]]:
                        m.start()
                    if kind == "sea":
                        get.start(12)
            acc_ref[...] += mm(jax.nn.gelu(pre).astype(BF16), wout_ref[h, cols])

    s = acc_ref[...].astype(BF16)
    if kind == "sea":
        to_quad(put(0), (s.astype(F32) * column(along(p_ref, WET))).astype(BF16))
        put.send(0)
        through.wait()
        return
    to_quad(put(0), s)
    put.send(0, wait=False)
    e = jnp.concatenate([p_ref[0, AIR_E:AIR_E + 4], p_ref[1, AIR_E:AIR_E + 4]], axis=1)
    e = jnp.concatenate([e, jnp.zeros((12, width), F32)], axis=0)
    fl = lax.dot_general(
        jnp.concatenate(thirds(e), axis=0), s, (((1,), (1,)), ((), ())),
        preferred_element_type=F32,
    )
    put(1)[...] = (fl[0:16] + fl[16:32] + fl[32:48])[0:8]
    if kind == "first":
        n = norm(s.astype(F32), wide(p_ref, AIR_G, half), wide(p_ref, AIR_S, half)).astype(BF16)
        to_chunks(ti_ref, n, xs, put, 2)
    put.done(0)


def sea_state(sea_ref, cols_ref, p_ref):
    cols = jnp.transpose(cols_ref[...])
    v = from_quad(sea_ref).astype(F32)
    for f in range(4):
        v = v + cols[:, f:f + 1] * wide(p_ref, SEA_E + f, sea_ref.shape[2])
    return v


def sea_kernel(get, put, scratch):
    r = get.raw(0)[0]
    p_ref = get(6)
    boxes = along(p_ref, BOX, 4).astype(jnp.int32)
    dr = (boxes >> 9) - r + 2
    here = lax.broadcasted_iota(jnp.int32, boxes.shape, 1)
    dc = ((boxes & (LONS - 1)) - here + (2 + LONS)) & (LONS - 1)
    where = dr * 8 + dc
    total = jnp.zeros((8, LONS), F32)
    for i in range(5):
        f = get.raw(1 + i)[...]
        for j in range(5):
            hits = jnp.sum(jnp.where(where == i * 8 + j, 1.0, 0.0), axis=0, keepdims=True)
            total = total + hits * pltpu.roll(f, (2 - j) % LONS, 1)
    put(1)[...] = total * 0.25
    sea_ref = get(7)
    half = sea_ref.shape[2]
    v = sea_state(sea_ref, put(1), p_ref)
    wet = column(along(p_ref, WET))
    n = (norm(v, wide(p_ref, SEA_G, half), wide(p_ref, SEA_S, half)) * wet).astype(BF16)
    to_chunks(get(8), n, scratch[0], put, 0)


def shape(dims, dtype):
    return jax.ShapeDtypeStruct(dims, dtype)


def chunk_scratch(half):
    return pltpu.VMEM((half // 128, 8 * ROWS, 128), F32)


class Inputs:
    def __init__(self, refs, moves):
        self.refs, self.moves, self.waited = refs, moves, set()

    def raw(self, i):
        return self.refs[i]

    def start(self, *which):
        for i in which:
            self.moves[i][0].start()

    def __call__(self, i):
        if i not in self.moves:
            return self.refs[i]
        move, buf = self.moves[i]
        if i not in self.waited:
            move.wait()
            self.waited.add(i)
        return buf


class Outputs:
    def __init__(self, refs, bufs, sems):
        self.refs, self.bufs, self.sems, self.moves = refs, bufs, sems, {}

    def raw(self, i):
        return self.refs[i]

    def sem(self, i):
        return self.sems.at[i]

    def __call__(self, i):
        return self.bufs.get(i, self.refs[i])

    def send(self, i, wait=True):
        self.moves[i] = pltpu.make_async_copy(self.bufs[i], self.refs[i], self.sems.at[i])
        self.moves[i].start()
        if wait:
            self.done(i)

    def done(self, i):
        self.moves[i].wait()


def call(body, name, args, outs, scratch, flops, limit=50):
    load = [i for i, (_, p) in enumerate(args) if p in "ld"]
    buffered = [i for i, (_, p) in enumerate(outs) if p == "l"]
    spaces = {"s": pltpu.SMEM, "v": pltpu.VMEM, "l": pltpu.HBM, "d": pltpu.HBM, "h": pltpu.HBM}
    n_in, n_out, n_load, n_buf = len(args), len(outs), len(load), len(buffered)

    def kernel(*refs):
        ins, results = refs[:n_in], refs[n_in:n_in + n_out]
        rest = refs[n_in + n_out:]
        in_bufs, out_bufs = rest[:n_load], rest[n_load:n_load + n_buf]
        in_sems, out_sems = rest[n_load + n_buf:n_load + n_buf + 2]
        moves = {}
        for k, i in enumerate(load):
            move = pltpu.make_async_copy(ins[i], in_bufs[k], in_sems.at[k])
            if args[i][1] == "l":
                move.start()
            moves[i] = (move, in_bufs[k])
        body(
            Inputs(ins, moves),
            Outputs(results, dict(zip(buffered, out_bufs)), out_sems),
            rest[n_load + n_buf + 2:],
        )

    arrays = [a for a, _ in args]
    return pl.pallas_call(
        kernel,
        out_shape=tuple(o for o, _ in outs),
        in_specs=[pl.BlockSpec(memory_space=spaces[p]) for _, p in args],
        out_specs=tuple(pl.BlockSpec(memory_space=spaces[p]) for _, p in outs),
        scratch_shapes=[
            *[pltpu.VMEM(arrays[i].shape, arrays[i].dtype) for i in load],
            *[pltpu.VMEM(outs[i][0].shape, outs[i][0].dtype) for i in buffered],
            pltpu.SemaphoreType.DMA((max(n_load, 1),)),
            pltpu.SemaphoreType.DMA((12,)),
            *scratch,
        ],
        compiler_params=pltpu.CompilerParams(vmem_limit_bytes=limit * 1024 * 1024),
        cost_estimate=pl.CostEstimate(
            flops=flops, bytes_accessed=sum(a.size * a.dtype.itemsize for a in arrays), transcendentals=0
        ),
        name=name,
    )(*arrays)


def run_modes(first, dev, x, packed, tables, w):
    half = x.shape[1]
    return call(
        functools.partial(modes_kernel, first), "modes",
        [(dev, "s"), (x, "v"), (packed, "l"), (tables, "h"), (w, "h")],
        [(shape((8 * ROWS, half), BF16), "l")],
        [
            chunk_scratch(half), chunk_scratch(half), pltpu.VMEM((6 * 256, 256), BF16),
            pltpu.VMEM(w.shape, BF16), pltpu.SemaphoreType.DMA((4,)), pltpu.SemaphoreType.DMA((4,)),
        ],
        8 * 512 * 4 * half * half * 2,
    )[0]


def run_grid(kind, place, x, v, packed, ti, w_in, w_out, *rest):
    half = x.shape[1]
    width = 2 * half
    outs = [(shape((4, LONS // 2, half), BF16), "l")]
    if kind != "sea":
        outs.append((shape((8, LONS), F32), "v"))
    if kind == "first":
        outs.append((shape((8 * ROWS, half), BF16), "l"))
    if kind == "sea":
        outs.append((shape(rest[1].shape, BF16), "h"))
    return call(
        functools.partial(grid_kernel, kind), "grid_" + kind,
        [
            (place, "s"), (x, "v"), (v, "d"), (packed, "d"), (ti, "v"),
            *[(a, "h") for a in (*w_in, *w_out)],
            *[(a, "d" if kind == "sea" else "h") for a in rest],
        ],
        outs,
        [
            chunk_scratch(half),
            pltpu.VMEM((LONS, width), BF16),
            pltpu.VMEM((LONS, width), F32),
            pltpu.VMEM((2, *w_in[0].shape), BF16),
            pltpu.VMEM((2, *w_out[0].shape), BF16),
            pltpu.SemaphoreType.DMA((6,)),
        ],
        8 * LONS * width * w_in[0].shape[1],
    )


def ring(x, by):
    return lax.ppermute(x, ("yh", "yl"), [(i, (i + by) % 4) for i in range(4)])


def swap_cores(x):
    return lax.ppermute(x, "comp", [(0, 1), (1, 0)])


def gather_weights(zero, w_in, w_out):
    comp = lax.axis_index("comp")
    out = []
    for w, by in ((w_in, 1), (w_out, -1)):
        n = w.shape[0] // 2
        here = ring(lax.dynamic_slice_in_dim(w, comp * n + zero, n, axis=0), by)
        out.append((w, here, swap_cores(here)))
    return out


def spread(x):
    half = x.shape[1]
    y = lax.all_to_all(x.reshape(ROWS, 8, half), ROW_AXES, 0, 0, tiled=True)
    return y.reshape(8 * ROWS, half)


def row_shift(x, by):
    def place(r):
        return (r // 2 % 2) * (ROWS // 2) + (r // 4) * 2 + r % 2

    return lax.ppermute(x, AXES, [(place(r), place((r + by) % ROWS)) for r in range(ROWS)])


def per_device(
    air, sea, wet, boxes,
    a_gain, a_shift, a_spec, a_sbias, a_win, a_bin, a_wout,
    s_gain, s_shift, s_spec, s_sbias, s_win, s_bin, s_wout,
    air_ex, sea_ex, skin, warm,
):
    lat = as_bf16(lat_tables())
    table = lon_table()
    tf = as_bf16(np.concatenate([table, table.T]))
    row = lax.axis_index(ROW_AXES).astype(jnp.int32).reshape(1)
    half = air.shape[2]
    sea_half = sea.shape[2]

    def fit(p):
        p = p.astype(F32)
        return jnp.pad(p, [(0, 0)] * (p.ndim - 1) + [(0, half - p.shape[-1])])

    place = jnp.stack([lax.axis_index("comp"), lax.axis_index("yl")]).astype(jnp.int32)
    air_plus, spec, part = call(
        pack_kernel, "pack",
        [
            (air, "l"), (sea, "l"), (skin[None], "v"),
            (a_gain, "v"), (wet, "v"), (a_spec, "l"), (s_spec, "l"), (a_shift, "v"), (warm[None], "v"),
        ],
        [
            (shape((4, LONS // 2 + PLUS, half), BF16), "h"), (shape((4, 640, 128), BF16), "l"),
            (shape((2, 640, 128), BF16), "l"),
        ],
        [pltpu.VMEM((4, PLUS, half), BF16), pltpu.SemaphoreType.DMA((2,))],
        2 * 16 * 1024 * sea_half,
    )
    air_rows = lax.all_to_all(air_plus, QUAD, 0, 0, tiled=True)

    near = lax.ppermute(part, "yl", [(0, 1), (1, 0)])
    after = part[0, 0, 0].astype(F32) * 0.0
    common = jnp.concatenate(
        [
            a_gain + after, a_shift, a_sbias.reshape(4, half), jnp.transpose(air_ex), warm[None],
            fit(a_bin.reshape(4, half)),
            fit(s_gain), fit(s_shift), fit(s_sbias.reshape(4, sea_half)), fit(sea_ex),
            fit(s_bin.reshape(4, sea_half)),
        ],
        axis=0,
    )
    comp, yl = lax.axis_index("comp"), lax.axis_index("yl")
    far = lax.ppermute(common, "yl", [(0, 1), (1, 0)])
    sides = jnp.where(yl == 0, jnp.stack([common, far]), jnp.stack([far, common]))
    cells = jnp.concatenate([fit(wet)[:, None], fit(jnp.transpose(boxes, (1, 0, 2)))], axis=1)
    mine = lax.dynamic_index_in_dim(cells, 2 * comp + yl, 0, keepdims=False)
    theirs = swap_cores(lax.dynamic_index_in_dim(cells, 2 * (1 - comp) + yl, 0, keepdims=False))
    cells = jnp.where(comp == 0, jnp.stack([mine, theirs]), jnp.stack([theirs, mine]))
    packed = jnp.concatenate([sides, cells], axis=1)

    aw, sw = call(
        weights_kernel, "weights", [(place, "s"), (spec, "v"), (near, "v"), (swap_cores(near), "v")],
        [
            (shape((2, 2, 2 * half, 2 * half), BF16), "l"),
            (shape((2, 2, 2 * sea_half, 2 * sea_half), BF16), "l"),
        ],
        [], 4_000_000_000,
    )
    zero = (packed[0, 0, 0] * 0.0 + near[0, 0, 0].astype(F32) * 0.0).astype(jnp.int32)
    awin, awout = gather_weights(zero, a_win, a_wout)
    swin, swout = gather_weights(zero, s_win, s_wout)
    sea_rows = lax.all_to_all(sea, QUAD, 0, 0, tiled=True)

    (x,) = call(
        start_kernel, "start", [(air_rows, "v"), (tf, "v")],
        [(shape((8 * ROWS, half), BF16), "l")], [chunk_scratch(half)], 4 * LONS * LONS * half,
    )
    x = spread(x)
    x = run_modes(AIR_C, row, x, packed, lat, aw)
    x = spread(x)
    s, flux_one, x = run_grid("first", place, x, air_rows, packed, tf, awin, awout)
    x = spread(x)
    x = run_modes(AIR_C, row, x, packed, lat, aw)
    x = spread(x)
    s, flux_two = run_grid("second", place, x, s, packed, tf, awin, awout, *swin[1:], *swout[1:], sea_rows)
    air_quad = lax.all_to_all(s, QUAD, 0, 0, tiled=True)

    flux = (flux_one + flux_two) / 2
    fluxes = (row_shift(flux, 2), row_shift(flux, 1), flux, row_shift(flux, -1), row_shift(flux, -2))
    x, cols = call(
        sea_kernel, "sea_start",
        [(row, "s"), *[(f, "v") for f in fluxes], (packed, "v"), (sea_rows, "v"), (tf, "v")],
        [(shape((8 * ROWS, sea_half), BF16), "l"), (shape((8, LONS), F32), "v")],
        [chunk_scratch(sea_half)], 4 * LONS * LONS * sea_half,
    )
    x = spread(x)
    x = run_modes(SEA_C, row, x, packed, lat, sw)
    x = spread(x)
    s, air_out = run_grid("sea", place, x, sea_rows, packed, tf, swin, swout, cols, air_quad)
    sea_out = lax.all_to_all(s, QUAD, 0, 0, tiled=True)
    return air_out, sea_out


def solution(mesh):
    fine = Mesh(mesh.devices.reshape(2, 4, 4, 2, 2), AXES)
    band = ("z", "x", "yh")
    placed = (
        P(band, "comp", "yl"),
        P(band, "comp", "yl"),
        P(band, "comp"),
        P(None, band, "comp"),
        P(None, "yl"),
        P(None, "yl"),
        P(None, "yl", None, None),
        P(None, "yl", None),
        P(None, "yl"),
        P("yl"),
        P("yl", None),
        P(None, "yl"),
        P(None, "yl"),
        P(None, "yl", None, None),
        P(None, "yl", None),
        P(None, "yl"),
        P("yl"),
        P("yl", None),
        P("yl", None),
        P(None, "yl"),
        P("yl"),
        P("yl"),
    )
    return jax.shard_map(
        per_device,
        mesh=fine,
        in_specs=placed,
        out_specs=(P(band, "comp", "yl"), P(band, "comp", "yl")),
        check_vma=False,
    )
```

```python
import functools
import math

import jax
import jax.numpy as jnp
import ml_dtypes
import numpy as np
from jax import lax
from jax.experimental import pallas as pl
from jax.experimental.pallas import tpu as pltpu
from jax.sharding import Mesh, PartitionSpec as P


ROWS = 128
LONS = 512
EPS = 1e-05
SHRINK = 0.01
F32 = jnp.float32
BF16 = jnp.bfloat16
AXES = ("comp", "z", "x", "yh", "yl")
ROW_AXES = ("z", "x", "yh", "comp", "yl")
QUAD = ("comp", "yl")

AIR_G, AIR_S, AIR_C, AIR_E, AIR_W, AIR_B = 0, 2, 5, 9, 13, 14
SEA_G, SEA_S, SEA_C, SEA_E, SEA_B = 18, 20, 23, 27, 31
WET, BOX, PACKED = 35, 36, 40
PLUS = 16


def lon_table():
    slot = np.arange(LONS // 2)
    w = np.arange(LONS)
    phase = 2.0 * np.pi * ((slot[:, None] * w[None, :]) % LONS) / LONS
    f = np.stack([np.cos(phase), -np.sin(phase)], axis=1)
    f[0, 1] = np.where(w % 2 == 0, 1.0, -1.0)
    f = f.reshape(ROWS, 4, LONS) / math.sqrt(LONS)
    return np.swapaxes(f, 0, 1).reshape(4 * ROWS, LONS)


def lat_tables():
    m = np.arange(ROWS)
    phase = 2.0 * np.pi * ((m[:, None] * m[None, :]) % ROWS) / ROWS
    c = np.cos(phase) / math.sqrt(ROWS)
    s = np.sin(phase) / math.sqrt(ROWS)
    o = np.zeros_like(c)
    usual = np.block([[c, s], [-s, c]])
    conj = np.block([[c, s], [s, -c]])
    first = np.stack(
        [np.concatenate([usual, conj]), np.block([[c, o], [-s, o], [o, c], [o, -s]])]
    )
    back = np.swapaxes(first, 1, 2)
    halves = np.stack([back[:, :, :256], back[:, :, 256:]], axis=1)
    return np.concatenate([first.reshape(-1, 256), halves.reshape(-1, 256), usual, usual.T])


def as_bf16(table):
    return jnp.asarray(np.ascontiguousarray(table).astype(ml_dtypes.bfloat16))


def mm(a, b):
    return jnp.dot(a, b, preferred_element_type=F32)


def norm(v, g, b):
    n = v.shape[1]
    m = jnp.sum(v, axis=1, keepdims=True) / n
    q = jnp.sum(v * v, axis=1, keepdims=True) / n
    return (v - m) * lax.rsqrt(q - m * m + EPS) * g + b


def from_quad(ref):
    return jnp.concatenate(
        [jnp.concatenate([ref[2 * c], ref[2 * c + 1]], axis=1) for c in range(2)], axis=0
    )


def to_quad(ref, x):
    w, half = x.shape[0] // 2, x.shape[1] // 2
    for c in range(2):
        for h in range(2):
            ref[2 * c + h] = x[c * w:(c + 1) * w, h * half:(h + 1) * half]


def wide(p_ref, i, half):
    return jnp.concatenate([p_ref[0, i:i + 1, :half], p_ref[1, i:i + 1, :half]], axis=1)


def along(p_ref, i, n=1):
    return jnp.concatenate([p_ref[0, i:i + n, :LONS // 2], p_ref[1, i:i + n, :LONS // 2]], axis=1)


def column(row):
    return jnp.transpose(jnp.broadcast_to(row, (8, row.shape[1])))[:, 0:1]


def to_chunks(tf_ref, n, scratch, put, i):
    half = n.shape[1] // 2
    for q in range(2):
        out = mm(tf_ref[:LONS], n[:, q * half:(q + 1) * half])
        for j in range(4):
            put_rows(scratch, 4 * q + j, out[j * ROWS:(j + 1) * ROWS])
    pour(put, i, scratch)


def put_rows(scratch, j, value):
    for t in range(scratch.shape[0]):
        scratch[t, pl.ds(j, ROWS, stride=8), :] = value[:, t * 128:(t + 1) * 128]


def pour(put, i, scratch):
    buf = put(i)
    moves = []
    for t in range(scratch.shape[0]):
        cols = slice(t * 128, (t + 1) * 128)
        buf[:, cols] = scratch[t].astype(BF16)
        moves.append(pltpu.make_async_copy(
            buf.at[:, pl.ds(t * 128, 128)], put.raw(i).at[:, pl.ds(t * 128, 128)], put.sem(8 + t)
        ))
        moves[-1].start()
    for m in moves:
        m.wait()


def fill(scratch, x_ref):
    for t in range(scratch.shape[0]):
        scratch[t] = x_ref[:, t * 128:(t + 1) * 128].astype(F32)


def rows_of(scratch, q, js):
    def one(j):
        return jnp.concatenate(
            [scratch[t, pl.ds(4 * q + j, ROWS, stride=8), :] for t in range(scratch.shape[0])], axis=1
        )

    return jnp.concatenate([one(j) for j in js], axis=0).astype(BF16)


def thirds(x):
    a = x.astype(BF16)
    r = x - a.astype(F32)
    b = r.astype(BF16)
    return a, b, (r - b.astype(F32)).astype(BF16)


def pack_kernel(get, put, scratch):
    out_hbm, (plus, sems) = put.raw(0), scratch
    air = get(0)
    n = air.shape[1]
    first = pltpu.make_async_copy(air, out_hbm.at[:, pl.ds(0, n)], sems.at[0])
    first.start()
    comp = lax.axis_index("comp")
    spec, part = put(1), put(2)
    spec[...] = jnp.zeros_like(spec)
    for src, top, k in ((5, 0, 96), (6, 384, 64)):
        for i in range(4):
            for j in range(4):
                spec[i, top + k * j:top + k * (j + 1), :k] = get(src)[i, j].astype(BF16)
    part[...] = spec[pl.ds(2 * comp, 2)]
    put.send(1, wait=False)
    put.send(2, wait=False)
    line = lambda ref: jnp.concatenate([ref[i:i + 1] for i in range(ref.shape[0])], axis=1)
    skin = line(get(2))
    skin = jnp.concatenate([*thirds(skin), jnp.zeros((13, skin.shape[1]), BF16)], axis=0)
    rest = jnp.concatenate([get(3)[0:1], get(7)[0:1], line(get(8))], axis=0)
    wet = get(4)[...].astype(F32)
    sea = get(1)
    half = rest.shape[1]
    pad = jnp.zeros((1, half - LONS // 2), F32)
    for r in range(4):
        t = lax.dot_general(skin, sea[r], (((1,), (1,)), ((), ())), preferred_element_type=F32)
        sst = jnp.concatenate([t[0:1] + t[1:2] + t[2:3], pad], axis=1)
        rows = jnp.concatenate([sst, jnp.concatenate([wet[r:r + 1], pad], axis=1), rest], axis=0)
        plus[r] = jnp.concatenate([*thirds(rows), jnp.zeros((1, half), BF16)], axis=0)
    last = pltpu.make_async_copy(plus, out_hbm.at[:, pl.ds(n, PLUS)], sems.at[1])
    last.start()
    last.wait()
    put.done(1)
    put.done(2)
    first.wait()


def plus_rows(air_ref, source):
    n = LONS // 2
    t = air_ref[source, n:n + PLUS].astype(F32)
    return t[0:5] + t[5:10] + t[10:15]


def air_state(air_ref):
    n = LONS // 2
    first = plus_rows(air_ref, 0)
    other = plus_rows(air_ref, 1)
    far = plus_rows(air_ref, 2)
    last = plus_rows(air_ref, 3)
    near_sst = (first[0:1, :n] + other[0:1, :n]) * first[1:2, :n]
    far_sst = (far[0:1, :n] + last[0:1, :n]) * far[1:2, :n]
    both = jnp.concatenate([first[2:5], other[2:5]], axis=1)
    air = jnp.concatenate(
        [jnp.concatenate([air_ref[2 * c, :n], air_ref[2 * c + 1, :n]], axis=1) for c in range(2)], axis=0
    )
    v = air.astype(F32) + column(jnp.concatenate([near_sst, far_sst], axis=1)) * both[2:3]
    return v, both


def start_kernel(get, put, scratch):
    v, both = air_state(get(0))
    n = norm(v, both[0:1], both[1:2]).astype(BF16)
    to_chunks(get(1), n, scratch[0], put, 0)


def weights_kernel(get, put, scratch):
    g_ref, near_ref, far_ref, aw_ref, sw_ref = get(1), get(2), get(3), put(0), put(1)
    comp, flip = get.raw(0)[0], get.raw(0)[1]
    for w_ref, top, k in ((aw_ref, 0, 96), (sw_ref, 384, 64)):
        half = 4 * k
        lane = lax.broadcasted_iota(jnp.int32, (128, half), 1)
        sub = lax.broadcasted_iota(jnp.int32, (128, half), 0)
        place = [jnp.where((lane == sub + k * n) & (sub < k), 1.0, 0.0).astype(BF16) for n in range(4)]
        for q in range(2):
            for layer in range(2):
                for part in range(2):
                    src = 2 * layer + part
                    own = g_ref[src, top:top + half]
                    far = jnp.where(
                        comp == layer, near_ref[part, top:top + half], far_ref[part, top:top + half]
                    )
                    here = jnp.where(flip == q, own, far)
                    block = jnp.concatenate(
                        [mm(here[k * n:k * (n + 1)], place[n]) for n in range(4)], axis=0
                    )
                    here = block.astype(BF16)
                    if part == 0:
                        w_ref[layer, q, :half, :half] = here
                        w_ref[layer, q, half:, half:] = here
                    else:
                        w_ref[layer, q, :half, half:] = here
                        w_ref[layer, q, half:, :half] = (-block).astype(BF16)
    put.send(0, wait=False)
    put.send(1)
    put.done(0)


def modes_kernel(first, get, put, scratch):
    dev_ref, x_ref = get.raw(0), get.raw(1)
    xs, os = scratch[:2]
    half = x_ref.shape[1]
    kind = jnp.where(dev_ref[0] == 0, 1, 0)
    t_buf, w_buf, t_sems, w_sems = scratch[2:]
    t_loads = []
    for i, (at, n) in enumerate(((512 * kind, 512), (2048, 256), (1024 + 512 * kind, 512), (2304, 256))):
        t_loads.append(pltpu.make_async_copy(
            get.raw(3).at[pl.ds(pl.multiple_of(at, 256), n)], t_buf.at[pl.ds((0, 512, 768, 1280)[i], n)],
            t_sems.at[i],
        ))
    loads = [
        [pltpu.make_async_copy(get.raw(4).at[i, q], w_buf.at[i, q], w_sems.at[2 * q + i]) for i in range(2)]
        for q in range(2)
    ]
    t_loads[0].start()
    t_loads[1].start()
    loads[0][0].start()
    fill(xs, get(1))
    t_loads[0].wait()
    t_loads[1].wait()
    t_loads[2].start()
    t_loads[3].start()
    loads[0][1].start()
    p_ref = get(2)
    for q in range(2):
        y0 = mm(t_buf[0:512], rows_of(xs, q, (0, 1))).astype(BF16)
        y1 = mm(t_buf[512:768], rows_of(xs, q, (2, 3))).astype(BF16)
        part = lambda y, i: y[i * ROWS:(i + 1) * ROWS]
        z = jnp.concatenate(
            [
                jnp.concatenate([part(y0, 0), part(y0, 1)], axis=1),
                jnp.concatenate([part(y0, 2), part(y0, 3)], axis=1),
                jnp.concatenate([part(y1, 0), part(y1, 1)], axis=1),
                jnp.concatenate([part(y1, 0), -part(y1, 1)], axis=1),
            ],
            axis=0,
        )
        bias = lambda i: jnp.concatenate(
            [p_ref[q, i:i + 1, :half], p_ref[q, i + 1:i + 2, :half]], axis=1
        )
        loads[q][0].wait()
        if q == 0:
            loads[1][0].start()
        o1 = jax.nn.relu(mm(z, w_buf[0, q]) + bias(first)).astype(BF16)
        loads[q][1].wait()
        if q == 0:
            loads[1][1].start()
            t_loads[2].wait()
            t_loads[3].wait()
        o2 = mm(o1, w_buf[1, q]) + bias(first + 2)
        f = o2 - jnp.clip(o2, -SHRINK, SHRINK)
        fr, fi = f[:, :half], f[:, half:]
        h0 = jnp.concatenate([part(fr, 0), part(fi, 0)], axis=0).astype(BF16)
        h2 = jnp.concatenate([part(fr, 1), part(fi, 1)], axis=0).astype(BF16)
        h1 = jnp.concatenate([part(fr, 2) + part(fr, 3), part(fi, 2) - part(fi, 3)], axis=0)
        b0 = mm(t_buf[768:1024], h0) + mm(t_buf[1024:1280], h2)
        b1 = mm(t_buf[1280:1536], h1.astype(BF16))
        for j, b in enumerate((part(b0, 0), part(b0, 1), part(b1, 0), part(b1, 1))):
            put_rows(os, 4 * q + j, b)
    pour(put, 0, os)


def grid_kernel(kind, get, put, scratch):
    place_ref, x_ref = get.raw(0), get.raw(1)
    xs, n2_ref, acc_ref, win_ref, wout_ref, sems = scratch
    half = x_ref.shape[1]
    width = 2 * half
    gains, shifts, bias = (SEA_G, SEA_S, SEA_B) if kind == "sea" else (AIR_G, AIR_S, AIR_B)
    comp, yl = place_ref[0], place_ref[1]
    piece = 512
    hid = win_ref.shape[2]
    pieces = hid // piece

    own, far = [], []
    for i, (buf, at) in enumerate(((win_ref, 5), (wout_ref, 8))):
        n = buf.shape[1] // 2
        part = lambda c: pl.ds(pl.multiple_of(c * n, n), n)
        own.append(pltpu.make_async_copy(get.raw(at), buf.at[0], sems.at[3 * i]))
        far.append([
            pltpu.make_async_copy(get.raw(at + 1), buf.at[1, part(comp)], sems.at[3 * i + 1]),
            pltpu.make_async_copy(get.raw(at + 2), buf.at[1, part(1 - comp)], sems.at[3 * i + 2]),
        ])

    get.start(2, 3)
    if kind == "sea":
        get.start(11)
    own[0].start()
    fill(xs, get(1))
    v_ref, p_ref, ti_ref = get(2), get(3), get(4)
    own[1].start()
    if kind == "first":
        v, _ = air_state(v_ref)
    elif kind == "second":
        v = from_quad(v_ref).astype(F32)
    else:
        v = sea_state(v_ref, get(11), p_ref)
    spatial = jnp.concatenate(
        [mm(ti_ref[LONS:], rows_of(xs, q, range(4))) for q in range(2)], axis=1
    )
    mixed = v + spatial
    n2_ref[...] = norm(mixed, wide(p_ref, gains + 1, half), wide(p_ref, shifts + 1, half)).astype(BF16)
    acc_ref[...] = mixed + wide(p_ref, shifts + 2, half)

    for h in range(2):
        if kind == "sea" and h == 1:
            through = pltpu.make_async_copy(get(12), put.raw(1), put.sem(1))
            through.start()
        source = yl if h == 0 else 1 - yl
        b_in = jnp.concatenate(
            [p_ref[source, bias + i:bias + i + 1, :hid // 4] for i in range(4)], axis=1
        )
        for i in range(pieces):
            cols = slice(i * piece, (i + 1) * piece)
            if i == 0:
                for m in far[0] if h else [own[0]]:
                    m.wait()
            pre = mm(n2_ref[...], win_ref[h, :, cols]) + b_in[:, cols]
            if i == 0:
                for m in far[1] if h else [own[1]]:
                    m.wait()
                if h == 0:
                    for m in [*far[0], *far[1]]:
                        m.start()
                    if kind == "sea":
                        get.start(12)
            acc_ref[...] += mm(jax.nn.gelu(pre).astype(BF16), wout_ref[h, cols])

    s = acc_ref[...].astype(BF16)
    if kind == "sea":
        to_quad(put(0), (s.astype(F32) * column(along(p_ref, WET))).astype(BF16))
        put.send(0)
        through.wait()
        return
    to_quad(put(0), s)
    put.send(0, wait=False)
    e = jnp.concatenate([p_ref[0, AIR_E:AIR_E + 4], p_ref[1, AIR_E:AIR_E + 4]], axis=1)
    e = jnp.concatenate([e, jnp.zeros((12, width), F32)], axis=0)
    fl = lax.dot_general(
        jnp.concatenate(thirds(e), axis=0), s, (((1,), (1,)), ((), ())),
        preferred_element_type=F32,
    )
    put(1)[...] = (fl[0:16] + fl[16:32] + fl[32:48])[0:8]
    if kind == "first":
        n = norm(s.astype(F32), wide(p_ref, AIR_G, half), wide(p_ref, AIR_S, half)).astype(BF16)
        to_chunks(ti_ref, n, xs, put, 2)
    put.done(0)


def sea_state(sea_ref, cols_ref, p_ref):
    cols = jnp.transpose(cols_ref[...])
    v = from_quad(sea_ref).astype(F32)
    for f in range(4):
        v = v + cols[:, f:f + 1] * wide(p_ref, SEA_E + f, sea_ref.shape[2])
    return v


def sea_kernel(get, put, scratch):
    r = get.raw(0)[0]
    p_ref = get(6)
    boxes = along(p_ref, BOX, 4).astype(jnp.int32)
    dr = (boxes >> 9) - r + 2
    here = lax.broadcasted_iota(jnp.int32, boxes.shape, 1)
    dc = ((boxes & (LONS - 1)) - here + (2 + LONS)) & (LONS - 1)
    where = dr * 8 + dc
    total = jnp.zeros((8, LONS), F32)
    for i in range(5):
        f = get.raw(1 + i)[...]
        for j in range(5):
            hits = jnp.sum(jnp.where(where == i * 8 + j, 1.0, 0.0), axis=0, keepdims=True)
            total = total + hits * pltpu.roll(f, (2 - j) % LONS, 1)
    put(1)[...] = total * 0.25
    sea_ref = get(7)
    half = sea_ref.shape[2]
    v = sea_state(sea_ref, put(1), p_ref)
    wet = column(along(p_ref, WET))
    n = (norm(v, wide(p_ref, SEA_G, half), wide(p_ref, SEA_S, half)) * wet).astype(BF16)
    to_chunks(get(8), n, scratch[0], put, 0)


def shape(dims, dtype):
    return jax.ShapeDtypeStruct(dims, dtype)


def chunk_scratch(half):
    return pltpu.VMEM((half // 128, 8 * ROWS, 128), F32)


class Inputs:
    def __init__(self, refs, moves):
        self.refs, self.moves, self.waited = refs, moves, set()

    def raw(self, i):
        return self.refs[i]

    def start(self, *which):
        for i in which:
            self.moves[i][0].start()

    def __call__(self, i):
        if i not in self.moves:
            return self.refs[i]
        move, buf = self.moves[i]
        if i not in self.waited:
            move.wait()
            self.waited.add(i)
        return buf


class Outputs:
    def __init__(self, refs, bufs, sems):
        self.refs, self.bufs, self.sems, self.moves = refs, bufs, sems, {}

    def raw(self, i):
        return self.refs[i]

    def sem(self, i):
        return self.sems.at[i]

    def __call__(self, i):
        return self.bufs.get(i, self.refs[i])

    def send(self, i, wait=True):
        self.moves[i] = pltpu.make_async_copy(self.bufs[i], self.refs[i], self.sems.at[i])
        self.moves[i].start()
        if wait:
            self.done(i)

    def done(self, i):
        self.moves[i].wait()


def call(body, name, args, outs, scratch, flops, limit=50):
    load = [i for i, (_, p) in enumerate(args) if p in "ld"]
    buffered = [i for i, (_, p) in enumerate(outs) if p == "l"]
    spaces = {"s": pltpu.SMEM, "v": pltpu.VMEM, "l": pltpu.HBM, "d": pltpu.HBM, "h": pltpu.HBM}
    n_in, n_out, n_load, n_buf = len(args), len(outs), len(load), len(buffered)

    def kernel(*refs):
        ins, results = refs[:n_in], refs[n_in:n_in + n_out]
        rest = refs[n_in + n_out:]
        in_bufs, out_bufs = rest[:n_load], rest[n_load:n_load + n_buf]
        in_sems, out_sems = rest[n_load + n_buf:n_load + n_buf + 2]
        moves = {}
        for k, i in enumerate(load):
            move = pltpu.make_async_copy(ins[i], in_bufs[k], in_sems.at[k])
            if args[i][1] == "l":
                move.start()
            moves[i] = (move, in_bufs[k])
        body(
            Inputs(ins, moves),
            Outputs(results, dict(zip(buffered, out_bufs)), out_sems),
            rest[n_load + n_buf + 2:],
        )

    arrays = [a for a, _ in args]
    return pl.pallas_call(
        kernel,
        out_shape=tuple(o for o, _ in outs),
        in_specs=[pl.BlockSpec(memory_space=spaces[p]) for _, p in args],
        out_specs=tuple(pl.BlockSpec(memory_space=spaces[p]) for _, p in outs),
        scratch_shapes=[
            *[pltpu.VMEM(arrays[i].shape, arrays[i].dtype) for i in load],
            *[pltpu.VMEM(outs[i][0].shape, outs[i][0].dtype) for i in buffered],
            pltpu.SemaphoreType.DMA((max(n_load, 1),)),
            pltpu.SemaphoreType.DMA((12,)),
            *scratch,
        ],
        compiler_params=pltpu.CompilerParams(vmem_limit_bytes=limit * 1024 * 1024),
        cost_estimate=pl.CostEstimate(
            flops=flops, bytes_accessed=sum(a.size * a.dtype.itemsize for a in arrays), transcendentals=0
        ),
        name=name,
    )(*arrays)


def run_modes(first, dev, x, packed, tables, w):
    half = x.shape[1]
    return call(
        functools.partial(modes_kernel, first), "modes",
        [(dev, "s"), (x, "v"), (packed, "l"), (tables, "h"), (w, "h")],
        [(shape((8 * ROWS, half), BF16), "l")],
        [
            chunk_scratch(half), chunk_scratch(half), pltpu.VMEM((6 * 256, 256), BF16),
            pltpu.VMEM(w.shape, BF16), pltpu.SemaphoreType.DMA((4,)), pltpu.SemaphoreType.DMA((4,)),
        ],
        8 * 512 * 4 * half * half * 2,
    )[0]


def run_grid(kind, place, x, v, packed, ti, w_in, w_out, *rest):
    half = x.shape[1]
    width = 2 * half
    outs = [(shape((4, LONS // 2, half), BF16), "l")]
    if kind != "sea":
        outs.append((shape((8, LONS), F32), "v"))
    if kind == "first":
        outs.append((shape((8 * ROWS, half), BF16), "l"))
    if kind == "sea":
        outs.append((shape(rest[1].shape, BF16), "h"))
    return call(
        functools.partial(grid_kernel, kind), "grid_" + kind,
        [
            (place, "s"), (x, "v"), (v, "d"), (packed, "d"), (ti, "v"),
            *[(a, "h") for a in (*w_in, *w_out)],
            *[(a, "d" if kind == "sea" else "h") for a in rest],
        ],
        outs,
        [
            chunk_scratch(half),
            pltpu.VMEM((LONS, width), BF16),
            pltpu.VMEM((LONS, width), F32),
            pltpu.VMEM((2, *w_in[0].shape), BF16),
            pltpu.VMEM((2, *w_out[0].shape), BF16),
            pltpu.SemaphoreType.DMA((6,)),
        ],
        8 * LONS * width * w_in[0].shape[1],
    )


def ring(x, by):
    return lax.ppermute(x, ("yh", "yl"), [(i, (i + by) % 4) for i in range(4)])


def swap_cores(x):
    return lax.ppermute(x, "comp", [(0, 1), (1, 0)])


def gather_weights(zero, w_in, w_out):
    comp = lax.axis_index("comp")
    out = []
    for w, by in ((w_in, 1), (w_out, -1)):
        n = w.shape[0] // 2
        here = ring(lax.dynamic_slice_in_dim(w, comp * n + zero, n, axis=0), by)
        out.append((w, here, swap_cores(here)))
    return out


def spread(x):
    half = x.shape[1]
    y = lax.all_to_all(x.reshape(ROWS, 8, half), ROW_AXES, 0, 0, tiled=True)
    return y.reshape(8 * ROWS, half)


def row_shift(x, by):
    def place(r):
        return (r // 2 % 2) * (ROWS // 2) + (r // 4) * 2 + r % 2

    return lax.ppermute(x, AXES, [(place(r), place((r + by) % ROWS)) for r in range(ROWS)])


def per_device(
    air, sea, wet, boxes,
    a_gain, a_shift, a_spec, a_sbias, a_win, a_bin, a_wout,
    s_gain, s_shift, s_spec, s_sbias, s_win, s_bin, s_wout,
    air_ex, sea_ex, skin, warm,
):
    lat = as_bf16(lat_tables())
    table = lon_table()
    tf = as_bf16(np.concatenate([table, table.T]))
    row = lax.axis_index(ROW_AXES).astype(jnp.int32).reshape(1)
    half = air.shape[2]
    sea_half = sea.shape[2]

    def fit(p):
        p = p.astype(F32)
        return jnp.pad(p, [(0, 0)] * (p.ndim - 1) + [(0, half - p.shape[-1])])

    place = jnp.stack([lax.axis_index("comp"), lax.axis_index("yl")]).astype(jnp.int32)
    air_plus, spec, part = call(
        pack_kernel, "pack",
        [
            (air, "l"), (sea, "l"), (skin.reshape(-1, 128), "l"), (a_gain, "l"), (wet, "l"),
            (a_spec, "l"), (s_spec, "l"), (a_shift, "l"), (warm.reshape(-1, 128), "l"),
        ],
        [
            (shape((4, LONS // 2 + PLUS, half), BF16), "h"), (shape((4, 640, 128), BF16), "l"),
            (shape((2, 640, 128), BF16), "l"),
        ],
        [pltpu.VMEM((4, PLUS, half), BF16), pltpu.SemaphoreType.DMA((2,))],
        2 * 16 * 1024 * sea_half, limit=56,
    )
    air_rows = lax.all_to_all(air_plus, QUAD, 0, 0, tiled=True)

    near = lax.ppermute(part, "yl", [(0, 1), (1, 0)])
    after = near[0, 0, 0].astype(F32) * 0.0
    common = jnp.concatenate(
        [
            a_gain + after, a_shift, a_sbias.reshape(4, half), jnp.transpose(air_ex), warm[None],
            fit(a_bin.reshape(4, half)),
            fit(s_gain), fit(s_shift), fit(s_sbias.reshape(4, sea_half)), fit(sea_ex),
            fit(s_bin.reshape(4, sea_half)),
        ],
        axis=0,
    )
    comp, yl = lax.axis_index("comp"), lax.axis_index("yl")
    far = lax.ppermute(common, "yl", [(0, 1), (1, 0)])
    sides = jnp.where(yl == 0, jnp.stack([common, far]), jnp.stack([far, common]))
    cells = jnp.concatenate([fit(wet)[:, None], fit(jnp.transpose(boxes, (1, 0, 2)))], axis=1)
    mine = lax.dynamic_index_in_dim(cells, 2 * comp + yl, 0, keepdims=False)
    theirs = swap_cores(lax.dynamic_index_in_dim(cells, 2 * (1 - comp) + yl, 0, keepdims=False))
    cells = jnp.where(comp == 0, jnp.stack([mine, theirs]), jnp.stack([theirs, mine]))
    packed = jnp.concatenate([sides, cells], axis=1)

    aw, sw = call(
        weights_kernel, "weights", [(place, "s"), (spec, "v"), (near, "v"), (swap_cores(near), "v")],
        [
            (shape((2, 2, 2 * half, 2 * half), BF16), "l"),
            (shape((2, 2, 2 * sea_half, 2 * sea_half), BF16), "l"),
        ],
        [], 4_000_000_000,
    )
    zero = after.astype(jnp.int32)
    awin, awout = gather_weights(zero, a_win, a_wout)
    swin, swout = gather_weights(zero, s_win, s_wout)
    sea_rows = lax.all_to_all(sea, QUAD, 0, 0, tiled=True)

    (x,) = call(
        start_kernel, "start", [(air_rows, "v"), (tf, "v")],
        [(shape((8 * ROWS, half), BF16), "l")], [chunk_scratch(half)], 4 * LONS * LONS * half,
    )
    x = spread(x)
    x = run_modes(AIR_C, row, x, packed, lat, aw)
    x = spread(x)
    s, flux_one, x = run_grid("first", place, x, air_rows, packed, tf, awin, awout)
    x = spread(x)
    x = run_modes(AIR_C, row, x, packed, lat, aw)
    x = spread(x)
    s, flux_two = run_grid("second", place, x, s, packed, tf, awin, awout, *swin[1:], *swout[1:], sea_rows)
    air_quad = lax.all_to_all(s, QUAD, 0, 0, tiled=True)

    flux = (flux_one + flux_two) / 2
    fluxes = (row_shift(flux, 2), row_shift(flux, 1), flux, row_shift(flux, -1), row_shift(flux, -2))
    x, cols = call(
        sea_kernel, "sea_start",
        [(row, "s"), *[(f, "v") for f in fluxes], (packed, "v"), (sea_rows, "v"), (tf, "v"), (air_quad, "h")],
        [(shape((8 * ROWS, sea_half), BF16), "l"), (shape((8, LONS), F32), "v")],
        [chunk_scratch(sea_half)], 4 * LONS * LONS * sea_half,
    )
    x = spread(x)
    x = run_modes(SEA_C, row, x, packed, lat, sw)
    x = spread(x)
    s, air_out = run_grid("sea", place, x, sea_rows, packed, tf, swin, swout, cols, air_quad)
    sea_out = lax.all_to_all(s, QUAD, 0, 0, tiled=True)
    return air_out, sea_out


def solution(mesh):
    fine = Mesh(mesh.devices.reshape(2, 4, 4, 2, 2), AXES)
    band = ("z", "x", "yh")
    placed = (
        P(band, "comp", "yl"),
        P(band, "comp", "yl"),
        P(band, "comp"),
        P(None, band, "comp"),
        P(None, "yl"),
        P(None, "yl"),
        P(None, "yl", None, None),
        P(None, "yl", None),
        P(None, "yl"),
        P("yl"),
        P("yl", None),
        P(None, "yl"),
        P(None, "yl"),
        P(None, "yl", None, None),
        P(None, "yl", None),
        P(None, "yl"),
        P("yl"),
        P("yl", None),
        P("yl", None),
        P(None, "yl"),
        P("yl"),
        P("yl"),
    )
    return jax.shard_map(
        per_device,
        mesh=fine,
        in_specs=placed,
        out_specs=(P(band, "comp", "yl"), P(band, "comp", "yl")),
        check_vma=False,
    )
```

```python
import functools
import math

import jax
import jax.numpy as jnp
import ml_dtypes
import numpy as np
from jax import lax
from jax.experimental import pallas as pl
from jax.experimental.pallas import tpu as pltpu
from jax.sharding import Mesh, PartitionSpec as P


ROWS = 128
LONS = 512
EPS = 1e-05
SHRINK = 0.01
F32 = jnp.float32
BF16 = jnp.bfloat16
AXES = ("comp", "z", "x", "yh", "yl")
ROW_AXES = ("z", "x", "yh", "comp", "yl")
QUAD = ("comp", "yl")

AIR_G, AIR_S, AIR_C, AIR_E, AIR_W, AIR_B = 0, 2, 5, 9, 13, 14
SEA_G, SEA_S, SEA_C, SEA_E, SEA_B = 18, 20, 23, 27, 31
WET, BOX, PACKED = 35, 36, 40
PLUS = 16


def lon_table():
    slot = np.arange(LONS // 2)
    w = np.arange(LONS)
    phase = 2.0 * np.pi * ((slot[:, None] * w[None, :]) % LONS) / LONS
    f = np.stack([np.cos(phase), -np.sin(phase)], axis=1)
    f[0, 1] = np.where(w % 2 == 0, 1.0, -1.0)
    f = f.reshape(ROWS, 4, LONS) / math.sqrt(LONS)
    return np.swapaxes(f, 0, 1).reshape(4 * ROWS, LONS)


def lat_tables():
    m = np.arange(ROWS)
    phase = 2.0 * np.pi * ((m[:, None] * m[None, :]) % ROWS) / ROWS
    c = np.cos(phase) / math.sqrt(ROWS)
    s = np.sin(phase) / math.sqrt(ROWS)
    o = np.zeros_like(c)
    usual = np.block([[c, s], [-s, c]])
    conj = np.block([[c, s], [s, -c]])
    first = np.stack(
        [np.concatenate([usual, conj]), np.block([[c, o], [-s, o], [o, c], [o, -s]])]
    )
    back = np.swapaxes(first, 1, 2)
    halves = np.stack([back[:, :, :256], back[:, :, 256:]], axis=1)
    return np.concatenate([first.reshape(-1, 256), halves.reshape(-1, 256), usual, usual.T])


def as_bf16(table):
    return jnp.asarray(np.ascontiguousarray(table).astype(ml_dtypes.bfloat16))


def mm(a, b):
    return jnp.dot(a, b, preferred_element_type=F32)


def norm(v, g, b):
    n = v.shape[1]
    m = jnp.sum(v, axis=1, keepdims=True) / n
    q = jnp.sum(v * v, axis=1, keepdims=True) / n
    return (v - m) * lax.rsqrt(q - m * m + EPS) * g + b


def from_quad(ref):
    return jnp.concatenate(
        [jnp.concatenate([ref[2 * c], ref[2 * c + 1]], axis=1) for c in range(2)], axis=0
    )


def to_quad(ref, x):
    w, half = x.shape[0] // 2, x.shape[1] // 2
    for c in range(2):
        for h in range(2):
            ref[2 * c + h] = x[c * w:(c + 1) * w, h * half:(h + 1) * half]


def wide(p_ref, i, half):
    return jnp.concatenate([p_ref[0, i:i + 1, :half], p_ref[1, i:i + 1, :half]], axis=1)


def along(p_ref, i, n=1):
    return jnp.concatenate([p_ref[0, i:i + n, :LONS // 2], p_ref[1, i:i + n, :LONS // 2]], axis=1)


def column(row):
    return jnp.transpose(jnp.broadcast_to(row, (8, row.shape[1])))[:, 0:1]


def to_chunks(tf_ref, n, scratch, put, i):
    half = n.shape[1] // 2
    for q in range(2):
        out = mm(tf_ref[:LONS], n[:, q * half:(q + 1) * half])
        for j in range(4):
            put_rows(scratch, 4 * q + j, out[j * ROWS:(j + 1) * ROWS])
    pour(put, i, scratch)


def put_rows(scratch, j, value):
    for t in range(scratch.shape[0]):
        scratch[t, pl.ds(j, ROWS, stride=8), :] = value[:, t * 128:(t + 1) * 128]


def pour(put, i, scratch):
    buf = put(i)
    moves = []
    for t in range(scratch.shape[0]):
        cols = slice(t * 128, (t + 1) * 128)
        buf[:, cols] = scratch[t].astype(BF16)
        moves.append(pltpu.make_async_copy(
            buf.at[:, pl.ds(t * 128, 128)], put.raw(i).at[:, pl.ds(t * 128, 128)], put.sem(8 + t)
        ))
        moves[-1].start()
    for m in moves:
        m.wait()


def fill(scratch, x_ref):
    for t in range(scratch.shape[0]):
        scratch[t] = x_ref[:, t * 128:(t + 1) * 128].astype(F32)


def rows_of(scratch, q, js):
    def one(j):
        return jnp.concatenate(
            [scratch[t, pl.ds(4 * q + j, ROWS, stride=8), :] for t in range(scratch.shape[0])], axis=1
        )

    return jnp.concatenate([one(j) for j in js], axis=0).astype(BF16)


def thirds(x):
    a = x.astype(BF16)
    r = x - a.astype(F32)
    b = r.astype(BF16)
    return a, b, (r - b.astype(F32)).astype(BF16)


def pack_kernel(get, put, scratch):
    out_hbm, (plus, sems) = put.raw(0), scratch
    air = get(0)
    n = air.shape[1]
    first = pltpu.make_async_copy(air, out_hbm.at[:, pl.ds(0, n)], sems.at[0])
    first.start()
    comp = lax.axis_index("comp")
    spec, part = put(1), put(2)
    spec[...] = jnp.zeros_like(spec)
    for src, top, k in ((5, 0, 96), (6, 384, 64)):
        for i in range(4):
            for j in range(4):
                spec[i, top + k * j:top + k * (j + 1), :k] = get(src)[i, j].astype(BF16)
    part[...] = spec[pl.ds(2 * comp, 2)]
    put.send(1, wait=False)
    put.send(2, wait=False)
    line = lambda ref: jnp.concatenate([ref[i:i + 1] for i in range(ref.shape[0])], axis=1)
    skin = line(get(2))
    skin = jnp.concatenate([*thirds(skin), jnp.zeros((13, skin.shape[1]), BF16)], axis=0)
    rest = jnp.concatenate([get(3)[0:1], get(7)[0:1], line(get(8))], axis=0)
    wet = get(4)[...].astype(F32)
    sea = get(1)
    half = rest.shape[1]
    pad = jnp.zeros((1, half - LONS // 2), F32)
    for r in range(4):
        t = lax.dot_general(skin, sea[r], (((1,), (1,)), ((), ())), preferred_element_type=F32)
        sst = jnp.concatenate([t[0:1] + t[1:2] + t[2:3], pad], axis=1)
        rows = jnp.concatenate([sst, jnp.concatenate([wet[r:r + 1], pad], axis=1), rest], axis=0)
        plus[r] = jnp.concatenate([*thirds(rows), jnp.zeros((1, half), BF16)], axis=0)
    last = pltpu.make_async_copy(plus, out_hbm.at[:, pl.ds(n, PLUS)], sems.at[1])
    last.start()
    last.wait()
    put.done(1)
    put.done(2)
    first.wait()


def plus_rows(air_ref, source):
    n = LONS // 2
    t = air_ref[source, n:n + PLUS].astype(F32)
    return t[0:5] + t[5:10] + t[10:15]


def air_state(air_ref):
    n = LONS // 2
    first = plus_rows(air_ref, 0)
    other = plus_rows(air_ref, 1)
    far = plus_rows(air_ref, 2)
    last = plus_rows(air_ref, 3)
    near_sst = (first[0:1, :n] + other[0:1, :n]) * first[1:2, :n]
    far_sst = (far[0:1, :n] + last[0:1, :n]) * far[1:2, :n]
    both = jnp.concatenate([first[2:5], other[2:5]], axis=1)
    air = jnp.concatenate(
        [jnp.concatenate([air_ref[2 * c, :n], air_ref[2 * c + 1, :n]], axis=1) for c in range(2)], axis=0
    )
    v = air.astype(F32) + column(jnp.concatenate([near_sst, far_sst], axis=1)) * both[2:3]
    return v, both


def start_kernel(get, put, scratch):
    v, both = air_state(get(0))
    n = norm(v, both[0:1], both[1:2]).astype(BF16)
    to_chunks(get(1), n, scratch[0], put, 0)


def weights_kernel(get, put, scratch):
    g_ref, near_ref, far_ref, aw_ref, sw_ref = get(1), get(2), get(3), put(0), put(1)
    comp, flip = get.raw(0)[0], get.raw(0)[1]
    for w_ref, top, k in ((aw_ref, 0, 96), (sw_ref, 384, 64)):
        half = 4 * k
        lane = lax.broadcasted_iota(jnp.int32, (128, half), 1)
        sub = lax.broadcasted_iota(jnp.int32, (128, half), 0)
        place = [jnp.where((lane == sub + k * n) & (sub < k), 1.0, 0.0).astype(BF16) for n in range(4)]
        for q in range(2):
            for layer in range(2):
                for part in range(2):
                    src = 2 * layer + part
                    own = g_ref[src, top:top + half]
                    far = jnp.where(
                        comp == layer, near_ref[part, top:top + half], far_ref[part, top:top + half]
                    )
                    here = jnp.where(flip == q, own, far)
                    block = jnp.concatenate(
                        [mm(here[k * n:k * (n + 1)], place[n]) for n in range(4)], axis=0
                    )
                    here = block.astype(BF16)
                    if part == 0:
                        w_ref[layer, q, :half, :half] = here
                        w_ref[layer, q, half:, half:] = here
                    else:
                        w_ref[layer, q, :half, half:] = here
                        w_ref[layer, q, half:, :half] = (-block).astype(BF16)
    put.send(0, wait=False)
    put.send(1)
    put.done(0)


def modes_kernel(first, get, put, scratch):
    dev_ref, x_ref = get.raw(0), get.raw(1)
    xs, os = scratch[:2]
    half = x_ref.shape[1]
    kind = jnp.where(dev_ref[0] == 0, 1, 0)
    t_buf, w_buf, t_sems, w_sems = scratch[2:]
    t_loads = []
    for i, (at, n) in enumerate(((512 * kind, 512), (2048, 256), (1024 + 512 * kind, 512), (2304, 256))):
        t_loads.append(pltpu.make_async_copy(
            get.raw(3).at[pl.ds(pl.multiple_of(at, 256), n)], t_buf.at[pl.ds((0, 512, 768, 1280)[i], n)],
            t_sems.at[i],
        ))
    loads = [
        [pltpu.make_async_copy(get.raw(4).at[i, q], w_buf.at[i, q], w_sems.at[2 * q + i]) for i in range(2)]
        for q in range(2)
    ]
    t_loads[0].start()
    t_loads[1].start()
    loads[0][0].start()
    fill(xs, get(1))
    t_loads[0].wait()
    t_loads[1].wait()
    t_loads[2].start()
    t_loads[3].start()
    loads[0][1].start()
    p_ref = get(2)
    for q in range(2):
        y0 = mm(t_buf[0:512], rows_of(xs, q, (0, 1))).astype(BF16)
        y1 = mm(t_buf[512:768], rows_of(xs, q, (2, 3))).astype(BF16)
        part = lambda y, i: y[i * ROWS:(i + 1) * ROWS]
        z = jnp.concatenate(
            [
                jnp.concatenate([part(y0, 0), part(y0, 1)], axis=1),
                jnp.concatenate([part(y0, 2), part(y0, 3)], axis=1),
                jnp.concatenate([part(y1, 0), part(y1, 1)], axis=1),
                jnp.concatenate([part(y1, 0), -part(y1, 1)], axis=1),
            ],
            axis=0,
        )
        bias = lambda i: jnp.concatenate(
            [p_ref[q, i:i + 1, :half], p_ref[q, i + 1:i + 2, :half]], axis=1
        )
        loads[q][0].wait()
        if q == 0:
            loads[1][0].start()
        o1 = jax.nn.relu(mm(z, w_buf[0, q]) + bias(first)).astype(BF16)
        loads[q][1].wait()
        if q == 0:
            loads[1][1].start()
            t_loads[2].wait()
            t_loads[3].wait()
        o2 = mm(o1, w_buf[1, q]) + bias(first + 2)
        f = o2 - jnp.clip(o2, -SHRINK, SHRINK)
        fr, fi = f[:, :half], f[:, half:]
        h0 = jnp.concatenate([part(fr, 0), part(fi, 0)], axis=0).astype(BF16)
        h2 = jnp.concatenate([part(fr, 1), part(fi, 1)], axis=0).astype(BF16)
        h1 = jnp.concatenate([part(fr, 2) + part(fr, 3), part(fi, 2) - part(fi, 3)], axis=0)
        b0 = mm(t_buf[768:1024], h0) + mm(t_buf[1024:1280], h2)
        b1 = mm(t_buf[1280:1536], h1.astype(BF16))
        for j, b in enumerate((part(b0, 0), part(b0, 1), part(b1, 0), part(b1, 1))):
            put_rows(os, 4 * q + j, b)
    pour(put, 0, os)


def grid_kernel(kind, get, put, scratch):
    place_ref, x_ref = get.raw(0), get.raw(1)
    xs, n2_ref, acc_ref, win_ref, wout_ref, sems = scratch
    half = x_ref.shape[1]
    width = 2 * half
    gains, shifts, bias = (SEA_G, SEA_S, SEA_B) if kind == "sea" else (AIR_G, AIR_S, AIR_B)
    comp, yl = place_ref[0], place_ref[1]
    piece = 512
    hid = win_ref.shape[2]
    pieces = hid // piece

    own, far = [], []
    for i, (buf, at) in enumerate(((win_ref, 5), (wout_ref, 8))):
        n = buf.shape[1] // 2
        part = lambda c: pl.ds(pl.multiple_of(c * n, n), n)
        own.append(pltpu.make_async_copy(get.raw(at), buf.at[0], sems.at[3 * i]))
        far.append([
            pltpu.make_async_copy(get.raw(at + 1), buf.at[1, part(comp)], sems.at[3 * i + 1]),
            pltpu.make_async_copy(get.raw(at + 2), buf.at[1, part(1 - comp)], sems.at[3 * i + 2]),
        ])

    get.start(2, 3)
    if kind == "sea":
        get.start(11)
    own[0].start()
    fill(xs, get(1))
    v_ref, p_ref, ti_ref = get(2), get(3), get(4)
    own[1].start()
    if kind == "first":
        v, _ = air_state(v_ref)
    elif kind == "second":
        v = from_quad(v_ref).astype(F32)
    else:
        v = sea_state(v_ref, get(11), p_ref)
    spatial = jnp.concatenate(
        [mm(ti_ref[LONS:], rows_of(xs, q, range(4))) for q in range(2)], axis=1
    )
    mixed = v + spatial
    n2_ref[...] = norm(mixed, wide(p_ref, gains + 1, half), wide(p_ref, shifts + 1, half)).astype(BF16)
    acc_ref[...] = mixed + wide(p_ref, shifts + 2, half)

    for h in range(2):
        if kind == "sea" and h == 1:
            through = pltpu.make_async_copy(get(12), put.raw(1), put.sem(1))
            through.start()
        source = yl if h == 0 else 1 - yl
        b_in = jnp.concatenate(
            [p_ref[source, bias + i:bias + i + 1, :hid // 4] for i in range(4)], axis=1
        )
        for i in range(pieces):
            cols = slice(i * piece, (i + 1) * piece)
            if i == 0:
                for m in far[0] if h else [own[0]]:
                    m.wait()
            pre = mm(n2_ref[...], win_ref[h, :, cols]) + b_in[:, cols]
            if i == 0:
                for m in far[1] if h else [own[1]]:
                    m.wait()
                if h == 0:
                    for m in [*far[0], *far[1]]:
                        m.start()
                    if kind == "sea":
                        get.start(12)
            acc_ref[...] += mm(jax.nn.gelu(pre).astype(BF16), wout_ref[h, cols])

    s = acc_ref[...].astype(BF16)
    if kind == "sea":
        to_quad(put(0), (s.astype(F32) * column(along(p_ref, WET))).astype(BF16))
        put.send(0)
        through.wait()
        return
    to_quad(put(0), s)
    put.send(0, wait=False)
    e = jnp.concatenate([p_ref[0, AIR_E:AIR_E + 4], p_ref[1, AIR_E:AIR_E + 4]], axis=1)
    e = jnp.concatenate([e, jnp.zeros((12, width), F32)], axis=0)
    fl = lax.dot_general(
        jnp.concatenate(thirds(e), axis=0), s, (((1,), (1,)), ((), ())),
        preferred_element_type=F32,
    )
    put(1)[...] = (fl[0:16] + fl[16:32] + fl[32:48])[0:8]
    if kind == "first":
        n = norm(s.astype(F32), wide(p_ref, AIR_G, half), wide(p_ref, AIR_S, half)).astype(BF16)
        to_chunks(ti_ref, n, xs, put, 2)
    put.done(0)


def sea_state(sea_ref, cols_ref, p_ref):
    cols = jnp.transpose(cols_ref[...])
    v = from_quad(sea_ref).astype(F32)
    for f in range(4):
        v = v + cols[:, f:f + 1] * wide(p_ref, SEA_E + f, sea_ref.shape[2])
    return v


def sea_kernel(get, put, scratch):
    r = get.raw(0)[0]
    p_ref = get(6)
    boxes = along(p_ref, BOX, 4).astype(jnp.int32)
    dr = (boxes >> 9) - r + 2
    here = lax.broadcasted_iota(jnp.int32, boxes.shape, 1)
    dc = ((boxes & (LONS - 1)) - here + (2 + LONS)) & (LONS - 1)
    where = dr * 8 + dc
    total = jnp.zeros((8, LONS), F32)
    for i in range(5):
        f = get.raw(1 + i)[...]
        for j in range(5):
            hits = jnp.sum(jnp.where(where == i * 8 + j, 1.0, 0.0), axis=0, keepdims=True)
            total = total + hits * pltpu.roll(f, (2 - j) % LONS, 1)
    put(1)[...] = total * 0.25
    sea_ref = get(7)
    half = sea_ref.shape[2]
    v = sea_state(sea_ref, put(1), p_ref)
    wet = column(along(p_ref, WET))
    n = (norm(v, wide(p_ref, SEA_G, half), wide(p_ref, SEA_S, half)) * wet).astype(BF16)
    to_chunks(get(8), n, scratch[0], put, 0)


def shape(dims, dtype):
    return jax.ShapeDtypeStruct(dims, dtype)


def chunk_scratch(half):
    return pltpu.VMEM((half // 128, 8 * ROWS, 128), F32)


class Inputs:
    def __init__(self, refs, moves):
        self.refs, self.moves, self.waited = refs, moves, set()

    def raw(self, i):
        return self.refs[i]

    def start(self, *which):
        for i in which:
            self.moves[i][0].start()

    def __call__(self, i):
        if i not in self.moves:
            return self.refs[i]
        move, buf = self.moves[i]
        if i not in self.waited:
            move.wait()
            self.waited.add(i)
        return buf


class Outputs:
    def __init__(self, refs, bufs, sems):
        self.refs, self.bufs, self.sems, self.moves = refs, bufs, sems, {}

    def raw(self, i):
        return self.refs[i]

    def sem(self, i):
        return self.sems.at[i]

    def __call__(self, i):
        return self.bufs.get(i, self.refs[i])

    def send(self, i, wait=True):
        self.moves[i] = pltpu.make_async_copy(self.bufs[i], self.refs[i], self.sems.at[i])
        self.moves[i].start()
        if wait:
            self.done(i)

    def done(self, i):
        self.moves[i].wait()


def call(body, name, args, outs, scratch, flops, limit=50):
    load = [i for i, (_, p) in enumerate(args) if p in "ld"]
    buffered = [i for i, (_, p) in enumerate(outs) if p == "l"]
    spaces = {"s": pltpu.SMEM, "v": pltpu.VMEM, "l": pltpu.HBM, "d": pltpu.HBM, "h": pltpu.HBM}
    n_in, n_out, n_load, n_buf = len(args), len(outs), len(load), len(buffered)

    def kernel(*refs):
        ins, results = refs[:n_in], refs[n_in:n_in + n_out]
        rest = refs[n_in + n_out:]
        in_bufs, out_bufs = rest[:n_load], rest[n_load:n_load + n_buf]
        in_sems, out_sems = rest[n_load + n_buf:n_load + n_buf + 2]
        moves = {}
        for k, i in enumerate(load):
            move = pltpu.make_async_copy(ins[i], in_bufs[k], in_sems.at[k])
            if args[i][1] == "l":
                move.start()
            moves[i] = (move, in_bufs[k])
        body(
            Inputs(ins, moves),
            Outputs(results, dict(zip(buffered, out_bufs)), out_sems),
            rest[n_load + n_buf + 2:],
        )

    arrays = [a for a, _ in args]
    return pl.pallas_call(
        kernel,
        out_shape=tuple(o for o, _ in outs),
        in_specs=[pl.BlockSpec(memory_space=spaces[p]) for _, p in args],
        out_specs=tuple(pl.BlockSpec(memory_space=spaces[p]) for _, p in outs),
        scratch_shapes=[
            *[pltpu.VMEM(arrays[i].shape, arrays[i].dtype) for i in load],
            *[pltpu.VMEM(outs[i][0].shape, outs[i][0].dtype) for i in buffered],
            pltpu.SemaphoreType.DMA((max(n_load, 1),)),
            pltpu.SemaphoreType.DMA((12,)),
            *scratch,
        ],
        compiler_params=pltpu.CompilerParams(vmem_limit_bytes=limit * 1024 * 1024),
        cost_estimate=pl.CostEstimate(
            flops=flops, bytes_accessed=sum(a.size * a.dtype.itemsize for a in arrays), transcendentals=0
        ),
        name=name,
    )(*arrays)


def run_modes(first, dev, x, packed, tables, w):
    half = x.shape[1]
    return call(
        functools.partial(modes_kernel, first), "modes",
        [(dev, "s"), (x, "v"), (packed, "l"), (tables, "h"), (w, "h")],
        [(shape((8 * ROWS, half), BF16), "l")],
        [
            chunk_scratch(half), chunk_scratch(half), pltpu.VMEM((6 * 256, 256), BF16),
            pltpu.VMEM(w.shape, BF16), pltpu.SemaphoreType.DMA((4,)), pltpu.SemaphoreType.DMA((4,)),
        ],
        8 * 512 * 4 * half * half * 2,
    )[0]


def run_grid(kind, place, x, v, packed, ti, w_in, w_out, *rest):
    half = x.shape[1]
    width = 2 * half
    outs = [(shape((4, LONS // 2, half), BF16), "l")]
    if kind != "sea":
        outs.append((shape((8, LONS), F32), "v"))
    if kind == "first":
        outs.append((shape((8 * ROWS, half), BF16), "l"))
    if kind == "sea":
        outs.append((shape(rest[1].shape, BF16), "h"))
    return call(
        functools.partial(grid_kernel, kind), "grid_" + kind,
        [
            (place, "s"), (x, "v"), (v, "d"), (packed, "d"), (ti, "v"),
            *[(a, "h") for a in (*w_in, *w_out)],
            *[(a, "d" if kind == "sea" else "h") for a in rest],
        ],
        outs,
        [
            chunk_scratch(half),
            pltpu.VMEM((LONS, width), BF16),
            pltpu.VMEM((LONS, width), F32),
            pltpu.VMEM((2, *w_in[0].shape), BF16),
            pltpu.VMEM((2, *w_out[0].shape), BF16),
            pltpu.SemaphoreType.DMA((6,)),
        ],
        8 * LONS * width * w_in[0].shape[1],
    )


def ring(x, by):
    return lax.ppermute(x, ("yh", "yl"), [(i, (i + by) % 4) for i in range(4)])


def swap_cores(x):
    return lax.ppermute(x, "comp", [(0, 1), (1, 0)])


def gather_weights(zero, w_in, w_out):
    comp = lax.axis_index("comp")
    out = []
    for w, by in ((w_in, 1), (w_out, -1)):
        n = w.shape[0] // 2
        here = ring(lax.dynamic_slice_in_dim(w, comp * n + zero, n, axis=0), by)
        out.append((w, here, swap_cores(here)))
    return out


def spread(x):
    half = x.shape[1]
    y = lax.all_to_all(x.reshape(ROWS, 8, half), ROW_AXES, 0, 0, tiled=True)
    return y.reshape(8 * ROWS, half)


def row_shift(x, by):
    def place(r):
        return (r // 2 % 2) * (ROWS // 2) + (r // 4) * 2 + r % 2

    return lax.ppermute(x, AXES, [(place(r), place((r + by) % ROWS)) for r in range(ROWS)])


def per_device(
    air, sea, wet, boxes,
    a_gain, a_shift, a_spec, a_sbias, a_win, a_bin, a_wout,
    s_gain, s_shift, s_spec, s_sbias, s_win, s_bin, s_wout,
    air_ex, sea_ex, skin, warm,
):
    lat = as_bf16(lat_tables())
    table = lon_table()
    tf = as_bf16(np.concatenate([table, table.T]))
    row = lax.axis_index(ROW_AXES).astype(jnp.int32).reshape(1)
    half = air.shape[2]
    sea_half = sea.shape[2]

    def fit(p):
        p = p.astype(F32)
        return jnp.pad(p, [(0, 0)] * (p.ndim - 1) + [(0, half - p.shape[-1])])

    place = jnp.stack([lax.axis_index("comp"), lax.axis_index("yl")]).astype(jnp.int32)
    air_plus, spec, part = call(
        pack_kernel, "pack",
        [
            (air, "l"), (sea, "l"), (skin.reshape(-1, 128), "l"), (a_gain, "l"), (wet, "l"),
            (a_spec, "l"), (s_spec, "l"), (a_shift, "l"), (warm.reshape(-1, 128), "l"),
        ],
        [
            (shape((4, LONS // 2 + PLUS, half), BF16), "h"), (shape((4, 640, 128), BF16), "l"),
            (shape((2, 640, 128), BF16), "l"),
        ],
        [pltpu.VMEM((4, PLUS, half), BF16), pltpu.SemaphoreType.DMA((2,))],
        2 * 16 * 1024 * sea_half, limit=56,
    )
    air_rows = lax.all_to_all(air_plus, QUAD, 0, 0, tiled=True)

    near = lax.ppermute(part, "yl", [(0, 1), (1, 0)])
    after = near[0, 0, 0].astype(F32) * 0.0
    common = jnp.concatenate(
        [
            a_gain + after, a_shift, a_sbias.reshape(4, half), jnp.transpose(air_ex), warm[None],
            fit(a_bin.reshape(4, half)),
            fit(s_gain), fit(s_shift), fit(s_sbias.reshape(4, sea_half)), fit(sea_ex),
            fit(s_bin.reshape(4, sea_half)),
        ],
        axis=0,
    )
    comp, yl = lax.axis_index("comp"), lax.axis_index("yl")
    far = lax.ppermute(common, "yl", [(0, 1), (1, 0)])
    sides = jnp.where(yl == 0, jnp.stack([common, far]), jnp.stack([far, common]))
    cells = jnp.concatenate([fit(wet)[:, None], fit(jnp.transpose(boxes, (1, 0, 2)))], axis=1)
    mine = lax.dynamic_index_in_dim(cells, 2 * comp + yl, 0, keepdims=False)
    theirs = swap_cores(lax.dynamic_index_in_dim(cells, 2 * (1 - comp) + yl, 0, keepdims=False))
    cells = jnp.where(comp == 0, jnp.stack([mine, theirs]), jnp.stack([theirs, mine]))
    packed = jnp.concatenate([sides, cells], axis=1)

    aw, sw = call(
        weights_kernel, "weights", [(place, "s"), (spec, "v"), (near, "v"), (swap_cores(near), "v")],
        [
            (shape((2, 2, 2 * half, 2 * half), BF16), "l"),
            (shape((2, 2, 2 * sea_half, 2 * sea_half), BF16), "l"),
        ],
        [], 4_000_000_000,
    )
    zero = (jnp.max(common) * 0.0).astype(jnp.int32)
    awin, awout = gather_weights(zero, a_win, a_wout)
    swin, swout = gather_weights(zero, s_win, s_wout)
    sea_rows = lax.all_to_all(sea, QUAD, 0, 0, tiled=True)

    (x,) = call(
        start_kernel, "start", [(air_rows, "v"), (tf, "v")],
        [(shape((8 * ROWS, half), BF16), "l")], [chunk_scratch(half)], 4 * LONS * LONS * half,
    )
    x = spread(x)
    x = run_modes(AIR_C, row, x, packed, lat, aw)
    x = spread(x)
    s, flux_one, x = run_grid("first", place, x, air_rows, packed, tf, awin, awout)
    x = spread(x)
    x = run_modes(AIR_C, row, x, packed, lat, aw)
    x = spread(x)
    s, flux_two = run_grid("second", place, x, s, packed, tf, awin, awout, *swin[1:], *swout[1:], sea_rows)
    air_quad = lax.all_to_all(s, QUAD, 0, 0, tiled=True)

    flux = (flux_one + flux_two) / 2
    fluxes = (row_shift(flux, 2), row_shift(flux, 1), flux, row_shift(flux, -1), row_shift(flux, -2))
    x, cols = call(
        sea_kernel, "sea_start",
        [(row, "s"), *[(f, "v") for f in fluxes], (packed, "v"), (sea_rows, "v"), (tf, "v"), (air_quad, "h")],
        [(shape((8 * ROWS, sea_half), BF16), "l"), (shape((8, LONS), F32), "v")],
        [chunk_scratch(sea_half)], 4 * LONS * LONS * sea_half,
    )
    x = spread(x)
    x = run_modes(SEA_C, row, x, packed, lat, sw)
    x = spread(x)
    s, air_out = run_grid("sea", place, x, sea_rows, packed, tf, swin, swout, cols, air_quad)
    sea_out = lax.all_to_all(s, QUAD, 0, 0, tiled=True)
    return air_out, sea_out


def solution(mesh):
    fine = Mesh(mesh.devices.reshape(2, 4, 4, 2, 2), AXES)
    band = ("z", "x", "yh")
    placed = (
        P(band, "comp", "yl"),
        P(band, "comp", "yl"),
        P(band, "comp"),
        P(None, band, "comp"),
        P(None, "yl"),
        P(None, "yl"),
        P(None, "yl", None, None),
        P(None, "yl", None),
        P(None, "yl"),
        P("yl"),
        P("yl", None),
        P(None, "yl"),
        P(None, "yl"),
        P(None, "yl", None, None),
        P(None, "yl", None),
        P(None, "yl"),
        P("yl"),
        P("yl", None),
        P("yl", None),
        P(None, "yl"),
        P("yl"),
        P("yl"),
    )
    return jax.shard_map(
        per_device,
        mesh=fine,
        in_specs=placed,
        out_specs=(P(band, "comp", "yl"), P(band, "comp", "yl")),
        check_vma=False,
    )
```
